512 devices in a mesh: dp: 4 (over z_lo), ctx: 32 (over y, x), tp: 4 (over z_hi, core).
Axes of the slice: x: 4, y: 8, z: 8 (z_hi: 2, z_lo: 4; z = z_hi * 4 + z_lo), core: 2. Of those that a mesh axis runs over, the one named last changes fastest.
Arguments:
- residual_in: bfloat16 [24576, 1536], P(('dp', 'ctx')), parts along dimension 0, may hold values from -11 to 11
- queries: bfloat16 [24576, 1536], P(('dp', 'ctx'), 'tp'), parts along dimension 0, may hold values from -9 to 9
- keys: bfloat16 [24576, 1536], P(('dp', 'ctx'), 'tp'), parts along dimension 0, may hold values from -9 to 9
- values: bfloat16 [24576, 1536], P(('dp', 'ctx'), 'tp'), parts along dimension 0, may hold values from -6 to 6
- out_weight: bfloat16 [1536, 1536], P('tp'), may hold values from -0.15625 to 0.15625
- norm_gain: float32 [1536], replicated, may hold values from 0.1 to 1.9
- norm_bias: float32 [1536], replicated, may hold values from -2.5 to 2.5
- glu_weight: bfloat16 [1536, 2, 1536], P(None, None, 'tp'), may hold values from -0.15625 to 0.15625
- conv_weight: float32 [31, 1536], P(None, 'tp'), may hold values from -1 to 1
- conv_scale: float32 [1536], P('tp'), may hold values from 0.1 to 1.9
- conv_shift: float32 [1536], P('tp'), may hold values from -2.5 to 2.5
Outputs:
- attended: bfloat16 [24576, 1536], P(('dp', 'ctx', 'tp')), parts along dimension 0
- conv_out: bfloat16 [24576, 1536], P(('dp', 'ctx'), 'tp'), parts along dimension 0
The draws below stay inside these ranges and needn't reach their ends.
There are 4 independent parts, one for each index of `dp`. The reference program is written for one: setup_inputs(seed, part) draws one part's arguments, and reference() takes and returns one part's arrays. A program takes and returns all parts, laid end to end along the dimension named above; an argument that names none is the same for every part. Nothing has to cross between parts.
All inputs are finite; a program needn't handle non-finite values.
Results may differ from the reference program's by a relative error of at most 0.008.
Values may be sent and summed in bfloat16 or wider, within the bound.
A program may use at most 64 MiB of HBM per device.

```python
import math
import jax
import jax.numpy as jnp
from jax import lax

D = 1536
HEADS = 16
KERNEL = 31
KEY_BLOCK = 64
HD = 96
SEQ = 6144


def draw_residual_in(key, part):
    own_key = jax.random.fold_in(key, 5)
    result = jax.random.truncated_normal(own_key, -4.0, 4.0, (SEQ, D), jnp.float32)
    return result.astype(jnp.bfloat16)


def draw_queries(key, part):
    own_key = jax.random.fold_in(key, 7)
    result = 1.6 * jax.random.truncated_normal(own_key, -4.0, 4.0, (SEQ, D), jnp.float32)
    return result.astype(jnp.bfloat16)


def draw_keys(key, part):
    own_key = jax.random.fold_in(key, 9)
    result = 1.6 * jax.random.truncated_normal(own_key, -4.0, 4.0, (SEQ, D), jnp.float32)
    return result.astype(jnp.bfloat16)


def level_of(rng, extent, pieces, low, top_value):
    def one(position, blocks):
        heights = jax.random.uniform(jax.random.fold_in(jax.random.fold_in(rng, 6), position), (blocks,), jnp.float32, low / len(pieces), top_value / len(pieces))
        return jnp.repeat(jnp.exp(heights), extent[position] // blocks).reshape((-1,) + (1,) * (len(extent) - position - 1))

    level = one(*pieces[0])
    for cut in pieces[1:]:
        level = level * one(*cut)
    return level


def scatter_about(key, dims, spread, bound, cuts=(), kind=jnp.bfloat16):
    values = jax.random.normal(key, dims, jnp.float32) * spread
    if len(cuts) > 0:
        values = level_of(key, dims, cuts, -0.22, 0.18) * values
    return jnp.clip(values, min=-bound, max=bound).astype(kind)


def setup_inputs(seed: int = 0, part: int = 0) -> dict:
    splits = jax.random.split(jax.random.key(seed), 12)
    part_splits = jax.random.split(jax.random.fold_in(splits[11], part), 12)
    return {
        "residual_in": draw_residual_in(jax.random.fold_in(jax.random.fold_in(splits[11], part), 71), part),
        "queries": draw_queries(jax.random.fold_in(jax.random.fold_in(splits[11], part), 71), part),
        "keys": draw_keys(jax.random.fold_in(jax.random.fold_in(splits[11], part), 71), part),
        "values": scatter_about(part_splits[3], (SEQ, D), 1.0, 6.0, ((0, 32), (1, 4))),
        "out_weight": scatter_about(splits[4], (D, D), D ** -0.5, 0.15625, ((0, 4),)),
        "norm_gain": jnp.clip(1.0 + 0.18 * jax.random.normal(splits[5], (D,), jnp.float32), 0.1, 1.9),
        "norm_bias": scatter_about(splits[6], (D,), 0.5, 2.5, (), jnp.float32),
        "glu_weight": scatter_about(splits[7], (D, 2, D), D ** -0.5, 0.15625, ((2, 4),)),
        "conv_weight": scatter_about(splits[8], (KERNEL, D), KERNEL ** -0.5, 1.0, ((1, 4),), jnp.float32),
        "conv_scale": jnp.clip(1.0 + 0.18 * jax.random.normal(splits[9], (D,), jnp.float32), 0.1, 1.9),
        "conv_shift": scatter_about(splits[10], (D,), 0.5, 2.5, ((0, 4),), jnp.float32),
    }


def head_attention(triple):
    query_rows, key_rows, value_rows = triple
    blocks = SEQ // KEY_BLOCK
    per_step = math.gcd(blocks, 16)
    inv_root = 1.0 / math.sqrt(HD)
    query_float = query_rows.astype(jnp.float32)
    key_groups = key_rows.astype(jnp.float32).reshape(blocks // per_step, per_step * KEY_BLOCK, HD)
    value_groups = value_rows.astype(jnp.float32).reshape(blocks // per_step, per_step, KEY_BLOCK, HD)

    def advance(carried, paired):
        top_score, weight_sum, mixture = carried
        key_part, value_part = paired
        scores = jnp.einsum('qd,kd->qk', query_float, key_part, precision=lax.Precision.HIGHEST) * inv_root
        scores = scores.reshape(SEQ, per_step, KEY_BLOCK)
        block_top = scores.max(-1)
        lifted = jnp.exp(scores - block_top[..., None])
        block_sums = lifted.sum(-1)
        weights = lax.optimization_barrier(lifted.astype(jnp.bfloat16)).astype(jnp.float32)
        block_mix = jnp.einsum('qgk,gkd->qgd', weights, value_part, precision=lax.Precision.HIGHEST)
        new_top = jnp.maximum(top_score, block_top.max(-1))
        carry_scale = jnp.exp(top_score - new_top)
        block_scale = jnp.exp(block_top - new_top[:, None])
        weight_sum = weight_sum * carry_scale + (block_sums * block_scale).sum(-1)
        mixture = mixture * carry_scale[:, None] + (block_mix * block_scale[..., None]).sum(1)
        return ((new_top, weight_sum, mixture), None)
    initial = (jnp.full((SEQ,), -1e+30, jnp.float32), jnp.zeros((SEQ,), jnp.float32), jnp.zeros((SEQ, HD), jnp.float32))
    final_state, unused = lax.scan(advance, initial, (key_groups, value_groups))
    return final_state[2] / final_state[1][:, None]

def layer_norm(source, norm_gain, norm_bias):
    rows_float = source.astype(jnp.float32)
    row_mean = rows_float.mean(-1, keepdims=True)
    centred = rows_float - row_mean
    row_var = (centred * centred).mean(-1, keepdims=True)
    return centred * lax.rsqrt(row_var + 1e-05) * norm_gain + norm_bias

def reference(residual_in, queries, keys, values, out_weight, norm_gain, norm_bias, glu_weight, conv_weight, conv_scale, conv_shift):

    def split_heads(matrix):
        return matrix.reshape(SEQ, HEADS, HD).transpose(1, 0, 2)
    per_head = lax.map(head_attention, (split_heads(queries), split_heads(keys), split_heads(values)))
    context = per_head.transpose(1, 0, 2).reshape(SEQ, D).astype(jnp.bfloat16)
    attended = (residual_in.astype(jnp.float32) + jnp.dot(context, out_weight, preferred_element_type=jnp.float32)).astype(jnp.bfloat16)
    normed = layer_norm(attended, norm_gain, norm_bias).astype(jnp.bfloat16)
    projected = jnp.dot(normed, glu_weight.reshape(D, 2 * D), preferred_element_type=jnp.float32)
    glu = (projected[:, :D] * jax.nn.sigmoid(projected[:, D:])).astype(jnp.bfloat16)
    rim_width = (KERNEL - 1) // 2
    padded = jnp.pad(glu, ((rim_width, rim_width), (0, 0)))
    conv_sum = jnp.zeros((SEQ, D), jnp.float32)
    for tap_index in range(KERNEL):
        conv_sum = conv_sum + padded[tap_index:tap_index + SEQ].astype(jnp.float32) * conv_weight[tap_index]
    shifted = conv_sum * conv_scale + conv_shift
    conv_out = (shifted * jax.nn.sigmoid(shifted)).astype(jnp.bfloat16)
    return (attended, conv_out)
```

```python
import functools
import math

import jax
import jax.numpy as jnp
from jax import lax
from jax.experimental import pallas as pl
from jax.experimental.pallas import tpu as pltpu
from jax.sharding import PartitionSpec as P

KERNEL = 31
HD = 96
LANES = 128
MESH = pl.DeviceIdType.MESH
F32 = jnp.float32
BF16 = jnp.bfloat16


def wait_for(ref, sem):
    pltpu.make_async_copy(ref, ref, sem).wait()


def send(src, dst, send_sem, recv_sem, device):
    pltpu.make_async_remote_copy(
        src_ref=src,
        dst_ref=dst,
        send_sem=send_sem,
        recv_sem=recv_sem,
        device_id=device,
        device_id_type=MESH,
    ).start()


def send_or_keep(here, src, dst, send_sem, recv_sem, device):
    @pl.when(here)
    def _():
        pltpu.make_async_copy(src, dst, recv_sem).start()

    @pl.when(jnp.logical_not(here))
    def _():
        send(src, dst, send_sem, recv_sem, device)


def kernel(
    ny,
    nx,
    resid_ref,
    q_ref,
    k_ref,
    v_ref,
    w_ref,
    gain_ref,
    bias_ref,
    glu_ref,
    taps_ref,
    scale_ref,
    shift_ref,
    att_ref,
    conv_ref,
    qs,
    kvs,
    qbuf,
    kvbuf,
    qfull,
    vfull,
    top,
    acc,
    accr,
    ctxs,
    cbuf,
    cat,
    wall,
    gw,
    resid,
    own,
    zs,
    zr,
    nbuf,
    gpad,
    hs,
    hr,
    sq_s,
    skv_s,
    q_r,
    qf_s,
    kv_r,
    xr_s,
    xl_s,
    xf_s,
    a_s,
    a_r,
    c_s,
    c_r,
    w_s,
    w_r,
    l_r,
    z_s,
    z_r,
    nz_s,
    ns_s,
    nf_s,
    n_r,
    h_s,
    h_r,
):
    half = ny // 2
    rows = q_ref.shape[0]
    block = rows // 4
    rim = gpad.shape[0] - rows
    rim = rim // 2
    width = conv_ref.shape[1]
    dp = lax.axis_index("dp")
    ctx = lax.axis_index("ctx")
    tp = lax.axis_index("tp")
    n_ctx = ny * nx
    y, x = ctx // nx, ctx % nx
    zh, core = tp // 2, tp % 2
    parity = y % 2

    def dev(yy, xx, tt):
        return (dp, yy * nx + xx, tt)

    sibling = (dp, ctx, zh * 2 + 1 - core)
    partner = (dp, ctx, (1 - zh) * 2 + core)
    x_right, x_left, x_far = (x + 1) % nx, (x + nx - 1) % nx, (x + 2) % nx
    right, left = dev(y, x_right, tp), dev(y, x_left, tp)

    barrier = pltpu.get_barrier_semaphore()

    def greet(device):
        pl.semaphore_signal(barrier, inc=1, device_id=device, device_id_type=MESH)

    for o in range(1, ny):
        for cc in range(2):
            greet(dev((y + o) % ny, x, zh * 2 + cc))
    greet(sibling)
    greet(partner)
    greet(right)
    greet(left)
    greet((dp, (ctx + 1) % n_ctx, tp))
    greet((dp, (ctx + n_ctx - 1) % n_ctx, tp))

    own_w = pltpu.make_async_copy(w_ref, wall.at[core], l_r.at[0])
    own_w.start()
    own_g = pltpu.make_async_copy(glu_ref, gw, l_r.at[1])
    own_g.start()
    own_x = pltpu.make_async_copy(
        resid_ref.at[pl.ds(pl.multiple_of(tp * block, block), block)], resid, l_r.at[2]
    )
    own_x.start()

    cut = rows * 3 // 4
    part = rows - cut
    for j in range(half):
        lo = HD * j
        kvs[j, 0:rows] = jnp.concatenate(
            [k_ref[:, lo : lo + HD], v_ref[:, lo : lo + 32]], axis=1
        )
        kvs[j, rows : rows + rows // 2] = jnp.concatenate(
            [v_ref[0 : rows // 2, lo + 32 : lo + HD], v_ref[rows // 2 : rows, lo + 32 : lo + HD]],
            axis=1,
        )
        qs[j] = jnp.concatenate(
            [
                q_ref[0:cut, lo : lo + HD],
                jnp.concatenate(
                    [q_ref[cut:rows, lo + 32 * i : lo + 32 * (i + 1)] for i in range(3)], axis=0
                ),
            ],
            axis=1,
        )

    pl.semaphore_wait(barrier, 2 * (ny - 1) + 6)

    for i in range(half):
        j = (y + i) % half
        head = core * half + j
        here = jnp.logical_and(head == y, core == parity)
        send_or_keep(
            here, qs.at[j], qbuf.at[y], sq_s.at[j], q_r.at[y], dev(head, x, zh * 2 + parity)
        )
    for i in range(half):
        j = (y + i) % half
        head = core * half + j
        here = jnp.logical_and(head == y, core == parity)
        send_or_keep(
            here,
            kvs.at[j],
            kvbuf.at[x, y // 2],
            skv_s.at[j],
            kv_r.at[x, y // 2],
            dev(head, x, zh * 2 + parity),
        )

    for i in range(half):
        ys = 2 * ((y // 2 + i) % half) + core
        wait_for(qbuf.at[ys], q_r.at[ys])
        send(qbuf.at[ys], qbuf.at[ys], qf_s.at[i], q_r.at[ys], sibling)
    for i in range(half):
        s = (y // 2 + i) % half
        wait_for(kvbuf.at[x, s], kv_r.at[x, s])
        send(kvbuf.at[x, s], kvbuf.at[x, s], xr_s.at[s], kv_r.at[x, s], right)
        send(kvbuf.at[x, s], kvbuf.at[x, s], xl_s.at[s], kv_r.at[x, s], left)
    send(w_ref, wall.at[core], w_s, w_r, sibling)
    for i in range(half):
        ys = 2 * ((y // 2 + i) % half) + 1 - core
        wait_for(qbuf.at[ys], q_r.at[ys])

    @pl.loop(0, ny)
    def _(t):
        base = pl.multiple_of(t * rows, rows)
        qfull[pl.ds(base, cut)] = jnp.concatenate(
            [qbuf[t, :, 0:HD], jnp.zeros((cut, LANES - HD), BF16)], axis=1
        )
        qfull[pl.ds(base + cut, part)] = jnp.concatenate(
            [qbuf[t, part * i : part * (i + 1), HD:LANES] for i in range(3)]
            + [jnp.zeros((part, LANES - HD), BF16)],
            axis=1,
        )

    factor = math.log2(math.e) / math.sqrt(HD)
    hr_rows = rows // 2
    keys = half * rows

    def unpack(slot):
        @pl.loop(0, half)
        def _(s):
            base = pl.multiple_of(s * rows, rows)
            ones = jnp.ones((hr_rows, LANES - HD), BF16)
            for b in range(2):
                vfull[pl.ds(base + b * hr_rows, hr_rows)] = jnp.concatenate(
                    [
                        kvbuf[slot, s, b * hr_rows : (b + 1) * hr_rows, HD:LANES],
                        kvbuf[slot, s, rows : rows + hr_rows, 64 * b : 64 * (b + 1)],
                        ones,
                    ],
                    axis=1,
                )

    def tile(slot, t, first):
        at = pl.ds(pl.multiple_of(t * rows, rows), rows)
        kk = kvbuf[slot, :, 0:rows, :].reshape(keys, LANES)
        s = lax.dot_general(
            qfull[at], kk, (((1,), (1,)), ((), ())), preferred_element_type=F32
        )
        peak = jnp.max(s, axis=1, keepdims=True) * factor
        if first:
            new = peak
        else:
            old = top[at][:, 0:1]
            new = jnp.maximum(old, peak)
        p = jnp.exp2(s * factor - new)
        mix = jnp.dot(p.astype(BF16), vfull[...], preferred_element_type=F32)
        if not first:
            mix = mix + acc[at] * jnp.exp2(old - new)
        return at, mix, new

    def attend(slot, first):
        unpack(slot)

        @pl.loop(0, ny)
        def _(t):
            at, mix, new = tile(slot, t, first)
            acc[at] = mix
            top[at] = jnp.broadcast_to(new, (rows, LANES))

    attend(x, True)
    for s in range(half):
        wait_for(kvbuf.at[x_left, s], kv_r.at[x_left, s])
        if s < half // 2:
            send(kvbuf.at[x_left, s], kvbuf.at[x_left, s], xf_s.at[s], kv_r.at[x_left, s], right)
    for s in range(half // 2, half):
        wait_for(kvbuf.at[x_right, s], kv_r.at[x_right, s])
        send(kvbuf.at[x_right, s], kvbuf.at[x_right, s], xf_s.at[s], kv_r.at[x_right, s], left)
    attend(x_left, False)
    for s in range(half // 2):
        wait_for(kvbuf.at[x_right, s], kv_r.at[x_right, s])
    attend(x_right, False)
    for s in range(half):
        wait_for(kvbuf.at[x_far, s], kv_r.at[x_far, s])
    unpack(x_far)
    lane = lax.broadcasted_iota(jnp.int32, (rows, LANES), 1)

    @pl.loop(0, half)
    def _(k):
        at, mix, new = tile(x_far, (1 - core) * half + k, False)
        acc[at] = jnp.where(lane >= LANES - 16, jnp.broadcast_to(new, (rows, LANES)), mix)
        send(acc.at[at], accr.at[k], a_s.at[k], a_r.at[k], sibling)

    @pl.loop(0, half)
    def _(k):
        at, mix, new = tile(x_far, core * half + k, False)
        wait_for(accr.at[k], a_r.at[k])
        other = accr[k]
        other_top = other[:, LANES - 1 : LANES]
        both = jnp.maximum(new, other_top)
        total = mix * jnp.exp2(new - both) + other * jnp.exp2(other_top - both)
        out = (total / total[:, HD : HD + 1]).astype(BF16)
        for cc in range(2):
            for zz in range(2):
                src = (zz * 2 + cc) * block
                ctxs[k, cc, zz * block : (zz + 1) * block] = out[src : src + block]
        yd = core * half + k
        for cc in range(2):
            send_or_keep(
                jnp.logical_and(yd == y, core == cc),
                ctxs.at[k, cc],
                cbuf.at[y],
                c_s.at[k, cc],
                c_r.at[y],
                dev(yd, x, zh * 2 + cc),
            )

    own_w.wait()
    own_x.wait()
    wait_for(wall.at[1 - core], w_r)
    for h in range(ny):
        wait_for(cbuf.at[h], c_r.at[h])
        cat[:, HD * h : HD * (h + 1)] = cbuf[h, :, 0:HD]

    def project(zz):
        return jnp.dot(
            cat[pl.ds(pl.multiple_of(zz * block, block), block)],
            wall[...].reshape(wall.shape[0] * wall.shape[1], wall.shape[2]),
            preferred_element_type=F32,
        )

    pieces = z_s.shape[0]
    step = block // pieces
    zs[...] = project(1 - zh).astype(BF16)
    for i in range(pieces):
        send(
            zs.at[pl.ds(i * step, step)],
            zr.at[pl.ds(i * step, step)],
            z_s.at[i],
            z_r.at[i],
            partner,
        )
    own[...] = project(zh) + resid[...].astype(F32)
    for i in range(pieces):
        piece = pl.ds(i * step, step)
        wait_for(zr.at[piece], z_r.at[i])
        attended = (own[piece] + zr[piece].astype(F32)).astype(BF16)
        att_ref[piece] = attended
        full = attended.astype(F32)
        centred = full - jnp.mean(full, axis=1, keepdims=True)
        var = jnp.mean(centred * centred, axis=1, keepdims=True)
        normed = centred * lax.rsqrt(var + 1e-05) * gain_ref[...].reshape(1, -1)
        nbuf[tp, piece] = (normed + bias_ref[...].reshape(1, -1)).astype(BF16)
        send(nbuf.at[tp, piece], nbuf.at[tp, piece], nz_s.at[i], n_r.at[tp, i], partner)
        send(nbuf.at[tp, piece], nbuf.at[tp, piece], ns_s.at[i], n_r.at[tp, i], sibling)

    def gate(zz):
        data = nbuf[pl.ds(zz * 2, 2)].reshape(2 * block, nbuf.shape[2])
        projected = jnp.dot(data, gw[...], preferred_element_type=F32)
        gated = projected[:, 0:width] * jax.nn.sigmoid(projected[:, width:])
        base = pl.multiple_of(rim + zz * 2 * block, 16)
        gpad[pl.ds(base, 2 * block)] = gated.astype(BF16).astype(F32)
        edge = pl.multiple_of(rim + zz * (rows - rim), 16)
        hs[zz] = gpad[pl.ds(edge, rim)].astype(BF16)
        target = ctx + 2 * zz - 1

        @pl.when(jnp.logical_and(target >= 0, target < n_ctx))
        def _():
            send(hs.at[zz], hr.at[1 - zz], h_s.at[zz], h_r.at[1 - zz], (dp, target, tp))

    own_g.wait()
    for i in range(pieces):
        wait_for(
            nbuf.at[zh * 2 + 1 - core, pl.ds(i * step, step)], n_r.at[zh * 2 + 1 - core, i]
        )
    gate(zh)
    tp_other = (1 - zh) * 2 + core
    for i in range(pieces):
        piece = pl.ds(i * step, step)
        wait_for(nbuf.at[tp_other, piece], n_r.at[tp_other, i])
        send(
            nbuf.at[tp_other, piece],
            nbuf.at[tp_other, piece],
            nf_s.at[i],
            n_r.at[tp_other, i],
            sibling,
        )
    for i in range(pieces):
        tp_last = (1 - zh) * 2 + 1 - core
        wait_for(nbuf.at[tp_last, pl.ds(i * step, step)], n_r.at[tp_last, i])
    gate(1 - zh)

    for side in range(2):
        source = ctx + 2 * side - 1
        exists = jnp.logical_and(source >= 0, source < n_ctx)
        place = pl.ds(side * (rim + rows), rim)

        @pl.when(exists)
        def _():
            wait_for(hr.at[side], h_r.at[side])
            gpad[place] = hr[side].astype(F32)

        @pl.when(jnp.logical_not(exists))
        def _():
            gpad[place] = jnp.zeros((rim, width), F32)

    offset = rim - (KERNEL - 1) // 2
    tall = 2 * rim
    taps = taps_ref[...]
    scale = scale_ref[...].reshape(1, -1)
    shift = shift_ref[...].reshape(1, -1)

    @pl.loop(0, rows // rim)
    def _(r):
        at = pl.multiple_of(r * rim, rim)
        window = gpad[pl.ds(at, rim + tall)]
        total = window[offset : offset + rim] * taps[0:1]
        for k in range(1, KERNEL):
            total = total + window[offset + k : offset + k + rim] * taps[k : k + 1]
        u = total * scale + shift
        conv_ref[pl.ds(at, rim)] = (u * jax.nn.sigmoid(u)).astype(BF16)

    for j in range(half):
        here = jnp.logical_and(core * half + j == y, core == parity)

        @pl.when(jnp.logical_not(here))
        def _():
            wait_for(qs.at[j], sq_s.at[j])
            wait_for(kvs.at[j], skv_s.at[j])

        wait_for(qbuf.at[j], qf_s.at[j])
        wait_for(kvbuf.at[x, j], xr_s.at[j])
        wait_for(kvbuf.at[x, j], xl_s.at[j])
        wait_for(kvbuf.at[x, j], xf_s.at[j])
        wait_for(accr.at[j], a_s.at[j])
        for cc in range(2):

            @pl.when(jnp.logical_not(jnp.logical_and(core * half + j == y, core == cc)))
            def _():
                wait_for(ctxs.at[j, cc], c_s.at[j, cc])

    wait_for(wall.at[core], w_s)
    for i in range(pieces):
        piece = pl.ds(i * step, step)
        wait_for(zs.at[piece], z_s.at[i])
        wait_for(nbuf.at[tp, piece], nz_s.at[i])
        wait_for(nbuf.at[tp, piece], ns_s.at[i])
        wait_for(nbuf.at[tp_other, piece], nf_s.at[i])
    for side in range(2):
        target = ctx + 2 * side - 1

        @pl.when(jnp.logical_and(target >= 0, target < n_ctx))
        def _():
            wait_for(hs.at[side], h_s.at[side])


def shards(
    n_ctx,
    residual_in,
    queries,
    keys,
    values,
    out_weight,
    norm_gain,
    norm_bias,
    glu_weight,
    conv_weight,
    conv_scale,
    conv_shift,
):
    rows, columns = queries.shape
    half = columns // HD
    ny = 2 * half
    nx = n_ctx // ny
    model = residual_in.shape[1]
    block = rows // 4
    pieces = block // 16
    rim = 16
    vmem = pl.BlockSpec(memory_space=pltpu.VMEM)
    anywhere = pl.BlockSpec(memory_space=pl.ANY)
    dma = pltpu.SemaphoreType.DMA
    tall = rows + rows // 2
    scratch = [
        pltpu.VMEM((half, rows * 3 // 4, LANES), BF16),
        pltpu.VMEM((half, tall, LANES), BF16),
        pltpu.VMEM((ny, rows * 3 // 4, LANES), BF16),
        pltpu.VMEM((nx, half, tall, LANES), BF16),
        pltpu.VMEM((ny * rows, LANES), BF16),
        pltpu.VMEM((half * rows, LANES), BF16),
        pltpu.VMEM((ny * rows, LANES), F32),
        pltpu.VMEM((ny * rows, LANES), F32),
        pltpu.VMEM((half, rows, LANES), F32),
        pltpu.VMEM((half, 2, 2 * block, LANES), BF16),
        pltpu.VMEM((ny, 2 * block, LANES), BF16),
        pltpu.VMEM((2 * block, ny * HD), BF16),
        pltpu.VMEM((2, half * HD, model), BF16),
        pltpu.VMEM((model, 2 * columns), BF16),
        pltpu.VMEM((block, model), BF16),
        pltpu.VMEM((block, model), F32),
        pltpu.VMEM((block, model), BF16),
        pltpu.VMEM((block, model), BF16),
        pltpu.VMEM((4, block, model), BF16),
        pltpu.VMEM((rows + 2 * rim, columns), F32),
        pltpu.VMEM((2, rim, columns), BF16),
        pltpu.VMEM((2, rim, columns), BF16),
        dma((half,)),
        dma((half,)),
        dma((ny,)),
        dma((half,)),
        dma((nx, half)),
        dma((half,)),
        dma((half,)),
        dma((half,)),
        dma((half,)),
        dma((half,)),
        dma((half, 2)),
        dma((ny,)),
        dma,
        dma,
        dma((3,)),
        dma((pieces,)),
        dma((pieces,)),
        dma((pieces,)),
        dma((pieces,)),
        dma((pieces,)),
        dma((4, pieces)),
        dma((2,)),
        dma((2,)),
    ]
    return pl.pallas_call(
        functools.partial(kernel, ny, nx),
        out_shape=(
            jax.ShapeDtypeStruct((block, model), BF16),
            jax.ShapeDtypeStruct((rows, columns), BF16),
        ),
        in_specs=[anywhere, vmem, vmem, vmem, anywhere, vmem, vmem, anywhere, vmem, vmem, vmem],
        out_specs=(vmem, vmem),
        scratch_shapes=scratch,
        compiler_params=pltpu.CompilerParams(
            collective_id=0, has_side_effects=True, vmem_limit_bytes=56 * 1024 * 1024
        ),
        cost_estimate=pl.CostEstimate(
            flops=3 * 10**9, bytes_accessed=10**7, transcendentals=5 * 10**6
        ),
    )(
        residual_in,
        queries,
        keys,
        values,
        out_weight,
        norm_gain,
        norm_bias,
        glu_weight.reshape(glu_weight.shape[0], 2 * columns),
        conv_weight,
        conv_scale,
        conv_shift,
    )


def solution(mesh):
    return jax.shard_map(
        functools.partial(shards, mesh.shape["ctx"]),
        mesh=mesh,
        in_specs=(
            P(("dp", "ctx"), None),
            P(("dp", "ctx"), "tp"),
            P(("dp", "ctx"), "tp"),
            P(("dp", "ctx"), "tp"),
            P("tp", None),
            P(),
            P(),
            P(None, None, "tp"),
            P(None, "tp"),
            P("tp"),
            P("tp"),
        ),
        out_specs=(P(("dp", "ctx", "tp"), None), P(("dp", "ctx"), "tp")),
        check_vma=False,
    )
```

```python
import functools
import math

import jax
import jax.numpy as jnp
from jax import lax
from jax.experimental import pallas as pl
from jax.experimental.pallas import tpu as pltpu
from jax.sharding import PartitionSpec as P

KERNEL = 31
HD = 96
LANES = 128
MESH = pl.DeviceIdType.MESH
F32 = jnp.float32
BF16 = jnp.bfloat16


def wait_for(ref, sem):
    pltpu.make_async_copy(ref, ref, sem).wait()


def send(src, dst, send_sem, recv_sem, device):
    pltpu.make_async_remote_copy(
        src_ref=src,
        dst_ref=dst,
        send_sem=send_sem,
        recv_sem=recv_sem,
        device_id=device,
        device_id_type=MESH,
    ).start()


def send_or_keep(here, src, dst, send_sem, recv_sem, device):
    @pl.when(here)
    def _():
        pltpu.make_async_copy(src, dst, recv_sem).start()

    @pl.when(jnp.logical_not(here))
    def _():
        send(src, dst, send_sem, recv_sem, device)


def kernel(
    ny,
    nx,
    resid_ref,
    q_ref,
    k_ref,
    v_ref,
    w_ref,
    gain_ref,
    bias_ref,
    glu_ref,
    att_ref,
    gpad,
    qs,
    kvs,
    qbuf,
    kvbuf,
    qfull,
    vfull,
    top,
    acc,
    accr,
    ctxs,
    cbuf,
    cat,
    wall,
    graw,
    gw,
    resid,
    own,
    zs,
    zr,
    nbuf,
    hs,
    hr,
    sq_s,
    skv_s,
    q_r,
    qf_s,
    kv_r,
    xr_s,
    xl_s,
    xf_s,
    a_s,
    a_r,
    c_s,
    c_r,
    w_s,
    w_r,
    l_r,
    z_s,
    z_r,
    nz_s,
    ns_s,
    nf_s,
    n_r,
    h_s,
    h_r,
):
    half = ny // 2
    rows = q_ref.shape[0]
    block = rows // 4
    rim = gpad.shape[0] - rows
    rim = rim // 2
    width = gpad.shape[1]
    dp = lax.axis_index("dp")
    ctx = lax.axis_index("ctx")
    tp = lax.axis_index("tp")
    n_ctx = ny * nx
    y, x = ctx // nx, ctx % nx
    zh, core = tp // 2, tp % 2
    parity = y % 2

    def dev(yy, xx, tt):
        return (dp, yy * nx + xx, tt)

    sibling = (dp, ctx, zh * 2 + 1 - core)
    partner = (dp, ctx, (1 - zh) * 2 + core)
    x_right, x_left, x_far = (x + 1) % nx, (x + nx - 1) % nx, (x + 2) % nx
    right, left = dev(y, x_right, tp), dev(y, x_left, tp)

    barrier = pltpu.get_barrier_semaphore()

    def greet(device):
        pl.semaphore_signal(barrier, inc=1, device_id=device, device_id_type=MESH)

    for o in range(1, ny):
        for cc in range(2):
            greet(dev((y + o) % ny, x, zh * 2 + cc))
    greet(sibling)
    greet(partner)
    greet(right)
    greet(left)
    greet((dp, (ctx + 1) % n_ctx, tp))
    greet((dp, (ctx + n_ctx - 1) % n_ctx, tp))

    own_w = pltpu.make_async_copy(w_ref, wall.at[core], l_r.at[0])
    own_w.start()
    own_g = pltpu.make_async_copy(glu_ref, graw, l_r.at[1])
    own_g.start()
    own_x = pltpu.make_async_copy(
        resid_ref.at[pl.ds(pl.multiple_of(tp * block, block), block)], resid, l_r.at[2]
    )
    own_x.start()

    cut = rows * 3 // 4
    part = rows - cut
    for j in range(half):
        lo = HD * j
        kvs[j, 0:rows] = jnp.concatenate(
            [k_ref[:, lo : lo + HD], v_ref[:, lo : lo + 32]], axis=1
        )
        kvs[j, rows : rows + rows // 2] = jnp.concatenate(
            [v_ref[0 : rows // 2, lo + 32 : lo + HD], v_ref[rows // 2 : rows, lo + 32 : lo + HD]],
            axis=1,
        )
        qs[j] = jnp.concatenate(
            [
                q_ref[0:cut, lo : lo + HD],
                jnp.concatenate(
                    [q_ref[cut:rows, lo + 32 * i : lo + 32 * (i + 1)] for i in range(3)], axis=0
                ),
            ],
            axis=1,
        )

    pl.semaphore_wait(barrier, 2 * (ny - 1) + 6)

    def rank(distance):
        sign = distance // (half + 1)
        fold = distance + sign * (ny - 2 * distance)
        odd = distance % 2
        return odd * (fold // 2 * 2 + sign) + (1 - odd) * (fold // 2 + fold // half + sign)

    near = [0]
    for o in range(1, half):
        near += [o, ny - o]
    near.append(half)

    def to_head(o, src, dst, send_sem, recv_sem):
        head = (y + o) % ny
        j = head % half
        device = dev(head, x, zh * 2 + parity)

        @pl.when(head // half == core)
        def _():
            if o == 0:
                send_or_keep(core == parity, src.at[j], dst, send_sem.at[j], recv_sem, device)
            else:
                send(src.at[j], dst, send_sem.at[j], recv_sem, device)

    for o in near[::-1]:
        to_head(o, qs, qbuf.at[y], sq_s, q_r.at[y])
    for o in near:
        place = rank((ny - o) % ny)
        to_head(o, kvs, kvbuf.at[x, place], skv_s, kv_r.at[x, place])

    for i in range(half):
        ys = 2 * ((y // 2 + i + 1) % half) + core
        wait_for(qbuf.at[ys], q_r.at[ys])
        send(qbuf.at[ys], qbuf.at[ys], qf_s.at[i], q_r.at[ys], sibling)
    send(w_ref, wall.at[core], w_s, w_r, sibling)
    own_g.wait()
    span = graw.shape[0] // half

    def spread(s):
        wait_for(kvbuf.at[x, s], kv_r.at[x, s])
        send(kvbuf.at[x, s], kvbuf.at[x, s], xr_s.at[s], kv_r.at[x, s], right)
        send(kvbuf.at[x, s], kvbuf.at[x, s], xl_s.at[s], kv_r.at[x, s], left)

    def pass_on(s):
        slot, target = (x_left, right) if s % 2 == 0 else (x_right, left)
        wait_for(kvbuf.at[slot, s], kv_r.at[slot, s])
        send(kvbuf.at[slot, s], kvbuf.at[slot, s], xf_s.at[s], kv_r.at[slot, s], target)

    def arrive(slot, s):
        wait_for(kvbuf.at[slot, s], kv_r.at[slot, s])

    def relayout(i):
        @pl.loop(0, span // 16)
        def _(r):
            at = pl.ds(pl.multiple_of(i * span + r * 16, 16), 16)
            pair = graw[at].astype(F32)
            gw[at] = jnp.concatenate([pair[:, 0, :], pair[:, 1, :]], axis=1).astype(BF16)

    spread(0)
    relayout(0)
    spread(1)
    relayout(1)
    relayout(2)
    pass_on(0)
    relayout(3)
    pass_on(1)
    for i in range(half):
        ys = 2 * ((y // 2 + i) % half) + 1 - core
        wait_for(qbuf.at[ys], q_r.at[ys])

    @pl.loop(0, ny)
    def _(t):
        base = pl.multiple_of(t * rows, rows)
        qfull[pl.ds(base, cut)] = jnp.concatenate(
            [qbuf[t, :, 0:HD], jnp.zeros((cut, LANES - HD), BF16)], axis=1
        )
        qfull[pl.ds(base + cut, part)] = jnp.concatenate(
            [qbuf[t, part * i : part * (i + 1), HD:LANES] for i in range(3)]
            + [jnp.zeros((part, LANES - HD), BF16)],
            axis=1,
        )

    factor = math.log2(math.e) / math.sqrt(HD)
    hr_rows = rows // 2
    tall = rows + hr_rows

    quarter = half // 2

    def unpack(slots, first_place):
        ones = jnp.ones((hr_rows, LANES - HD), BF16)
        for n, slot in enumerate(slots):
            for m in range(quarter):
                for b in range(2):
                    base = (n * quarter + m) * rows + b * hr_rows
                    vfull[base : base + hr_rows] = jnp.concatenate(
                        [
                            kvbuf[slot, first_place + m, b * hr_rows : (b + 1) * hr_rows, HD:LANES],
                            kvbuf[slot, first_place + m, rows:tall, 64 * b : 64 * (b + 1)],
                            ones,
                        ],
                        axis=1,
                    )

    wide = 2 * rows

    def tile(slots, place, base, first):
        at = pl.ds(pl.multiple_of(base, wide), wide)
        kk = jnp.concatenate(
            [
                kvbuf[slot, place : place + quarter, 0:rows, :].reshape(quarter * rows, LANES)
                for slot in slots
            ],
            axis=0,
        )
        s = lax.dot_general(
            qfull[at], kk, (((1,), (1,)), ((), ())), preferred_element_type=F32
        )
        peak = jnp.max(s, axis=1, keepdims=True) * factor
        if first:
            new = peak
        else:
            old = top[at][:, 0:1]
            new = jnp.maximum(old, peak)
        p = jnp.exp2(s * factor - new)
        mix = jnp.dot(p.astype(BF16), vfull[...], preferred_element_type=F32)
        if not first:
            mix = mix + acc[at] * jnp.exp2(old - new)
        return at, mix, new

    def attend(slots, place, first):
        unpack(slots, place)
        for t in range(half):
            at, mix, new = tile(slots, place, t * wide, first)
            acc[at] = mix
            top[at] = jnp.broadcast_to(new, (wide, LANES))

    arrive(x_left, 1)
    attend((x, x_left), 0, True)
    spread(2)
    arrive(x_right, 0)
    arrive(x_far, 0)
    arrive(x_far, 1)
    attend((x_right, x_far), 0, False)
    spread(3)
    pass_on(2)
    pass_on(3)
    arrive(x_left, 3)
    attend((x, x_left), 2, False)
    arrive(x_right, 2)
    arrive(x_far, 2)
    arrive(x_far, 3)
    last = (x_right, x_far)
    unpack(last, 2)
    lane = lax.broadcasted_iota(jnp.int32, (wide, LANES), 1)
    for t in range(half // 2):
        at, mix, new = tile(last, 2, (1 - core) * half * rows + t * wide, False)
        acc[at] = jnp.where(lane >= LANES - 16, jnp.broadcast_to(new, (wide, LANES)), mix)
        send(acc.at[at], accr.at[pl.ds(t * wide, wide)], a_s.at[t], a_r.at[t], sibling)
    for t in range(half // 2):
        at, mix, new = tile(last, 2, core * half * rows + t * wide, False)
        acc[at] = mix
        top[at] = jnp.broadcast_to(new, (wide, LANES))
    for t in range(half // 2):
        wait_for(accr.at[pl.ds(t * wide, wide)], a_r.at[t])
        for k in range(2 * t, 2 * t + 2):
            yd = core * half + k
            at = pl.ds(pl.multiple_of(yd * rows, rows), rows)
            other = accr[k * rows : (k + 1) * rows]
            other_top = other[:, LANES - 1 : LANES]
            new = top[at][:, 0:1]
            both = jnp.maximum(new, other_top)
            total = acc[at] * jnp.exp2(new - both) + other * jnp.exp2(other_top - both)
            out = (total / total[:, HD : HD + 1]).astype(BF16)
            for cc in range(2):
                for zz in range(2):
                    src = (zz * 2 + cc) * block
                    ctxs[k, cc, zz * block : (zz + 1) * block] = out[src : src + block]
            for cc in range(2):
                send_or_keep(
                    jnp.logical_and(yd == y, core == cc),
                    ctxs.at[k, cc],
                    cbuf.at[y],
                    c_s.at[k, cc],
                    c_r.at[y],
                    dev(yd, x, zh * 2 + cc),
                )

    own_w.wait()
    own_x.wait()
    wait_for(wall.at[1 - core], w_r)
    for h in range(ny):
        wait_for(cbuf.at[h], c_r.at[h])
        cat[:, HD * h : HD * (h + 1)] = cbuf[h, :, 0:HD]

    def project(zz):
        return jnp.dot(
            cat[pl.ds(pl.multiple_of(zz * block, block), block)],
            wall[...].reshape(wall.shape[0] * wall.shape[1], wall.shape[2]),
            preferred_element_type=F32,
        )

    pieces = z_s.shape[0]
    step = block // pieces
    zs[...] = project(1 - zh).astype(BF16)
    for i in range(pieces):
        send(
            zs.at[pl.ds(i * step, step)],
            zr.at[pl.ds(i * step, step)],
            z_s.at[i],
            z_r.at[i],
            partner,
        )
    own[...] = project(zh) + resid[...].astype(F32)
    for i in range(pieces):
        piece = pl.ds(i * step, step)
        wait_for(zr.at[piece], z_r.at[i])
        attended = (own[piece] + zr[piece].astype(F32)).astype(BF16)
        att_ref[piece] = attended
        full = attended.astype(F32)
        centred = full - jnp.mean(full, axis=1, keepdims=True)
        var = jnp.mean(centred * centred, axis=1, keepdims=True)
        normed = centred * lax.rsqrt(var + 1e-05) * gain_ref[...].reshape(1, -1)
        nbuf[tp, piece] = (normed + bias_ref[...].reshape(1, -1)).astype(BF16)
        send(nbuf.at[tp, piece], nbuf.at[tp, piece], nz_s.at[i], n_r.at[tp, i], partner)
        send(nbuf.at[tp, piece], nbuf.at[tp, piece], ns_s.at[i], n_r.at[tp, i], sibling)

    def gate(zz):
        data = nbuf[pl.ds(zz * 2, 2)].reshape(2 * block, nbuf.shape[2])
        projected = jnp.dot(data, gw[...], preferred_element_type=F32)
        gated = projected[:, 0:width] * jax.nn.sigmoid(projected[:, width:])
        base = pl.multiple_of(rim + zz * 2 * block, 16)
        gpad[pl.ds(base, 2 * block)] = gated.astype(BF16).astype(F32)
        edge = pl.multiple_of(rim + zz * (rows - rim), 16)
        hs[zz] = gpad[pl.ds(edge, rim)].astype(BF16)
        target = ctx + 2 * zz - 1

        @pl.when(jnp.logical_and(target >= 0, target < n_ctx))
        def _():
            send(hs.at[zz], hr.at[1 - zz], h_s.at[zz], h_r.at[1 - zz], (dp, target, tp))

    for i in range(pieces):
        wait_for(
            nbuf.at[zh * 2 + 1 - core, pl.ds(i * step, step)], n_r.at[zh * 2 + 1 - core, i]
        )
    gate(zh)
    tp_other = (1 - zh) * 2 + core
    for i in range(pieces):
        piece = pl.ds(i * step, step)
        wait_for(nbuf.at[tp_other, piece], n_r.at[tp_other, i])
        send(
            nbuf.at[tp_other, piece],
            nbuf.at[tp_other, piece],
            nf_s.at[i],
            n_r.at[tp_other, i],
            sibling,
        )
    for i in range(pieces):
        tp_last = (1 - zh) * 2 + 1 - core
        wait_for(nbuf.at[tp_last, pl.ds(i * step, step)], n_r.at[tp_last, i])
    gate(1 - zh)

    for side in range(2):
        source = ctx + 2 * side - 1
        exists = jnp.logical_and(source >= 0, source < n_ctx)
        place = pl.ds(side * (rim + rows), rim)

        @pl.when(exists)
        def _():
            wait_for(hr.at[side], h_r.at[side])
            gpad[place] = hr[side].astype(F32)

        @pl.when(jnp.logical_not(exists))
        def _():
            gpad[place] = jnp.zeros((rim, width), F32)

    for j in range(half):
        here = jnp.logical_and(core * half + j == y, core == parity)

        @pl.when(jnp.logical_not(here))
        def _():
            wait_for(qs.at[j], sq_s.at[j])
            wait_for(kvs.at[j], skv_s.at[j])

        wait_for(qbuf.at[j], qf_s.at[j])
        wait_for(kvbuf.at[x, j], xr_s.at[j])
        wait_for(kvbuf.at[x, j], xl_s.at[j])
        wait_for(kvbuf.at[x, j], xf_s.at[j])
        for cc in range(2):

            @pl.when(jnp.logical_not(jnp.logical_and(core * half + j == y, core == cc)))
            def _():
                wait_for(ctxs.at[j, cc], c_s.at[j, cc])

    wait_for(wall.at[core], w_s)
    for t in range(half // 2):
        wait_for(accr.at[pl.ds(t * wide, wide)], a_s.at[t])
    for i in range(pieces):
        piece = pl.ds(i * step, step)
        wait_for(zs.at[piece], z_s.at[i])
        wait_for(nbuf.at[tp, piece], nz_s.at[i])
        wait_for(nbuf.at[tp, piece], ns_s.at[i])
        wait_for(nbuf.at[tp_other, piece], nf_s.at[i])
    for side in range(2):
        target = ctx + 2 * side - 1

        @pl.when(jnp.logical_and(target >= 0, target < n_ctx))
        def _():
            wait_for(hs.at[side], h_s.at[side])


def convolve(att_in, gpad, taps_ref, scale_ref, shift_ref, att_ref, conv_ref):
    rows = conv_ref.shape[0]
    rim = (gpad.shape[0] - rows) // 2
    att_ref[...] = att_in[...]
    offset = rim - (KERNEL - 1) // 2
    taps = taps_ref[...]
    scale = scale_ref[...].reshape(1, -1)
    shift = shift_ref[...].reshape(1, -1)

    @pl.loop(0, rows // rim)
    def _(r):
        at = pl.multiple_of(r * rim, rim)
        window = gpad[pl.ds(at, 3 * rim)]
        total = window[offset : offset + rim] * taps[0:1]
        for k in range(1, KERNEL):
            total = total + window[offset + k : offset + k + rim] * taps[k : k + 1]
        u = total * scale + shift
        conv_ref[pl.ds(at, rim)] = (u * jax.nn.sigmoid(u)).astype(BF16)


def shards(
    n_ctx,
    residual_in,
    queries,
    keys,
    values,
    out_weight,
    norm_gain,
    norm_bias,
    glu_weight,
    conv_weight,
    conv_scale,
    conv_shift,
):
    rows, columns = queries.shape
    half = columns // HD
    ny = 2 * half
    nx = n_ctx // ny
    model = residual_in.shape[1]
    block = rows // 4
    pieces = block // 16
    rim = 16
    vmem = pl.BlockSpec(memory_space=pltpu.VMEM)
    anywhere = pl.BlockSpec(memory_space=pl.ANY)
    dma = pltpu.SemaphoreType.DMA
    tall = rows + rows // 2
    scratch = [
        pltpu.VMEM((half, rows * 3 // 4, LANES), BF16),
        pltpu.VMEM((half, tall, LANES), BF16),
        pltpu.VMEM((ny, rows * 3 // 4, LANES), BF16),
        pltpu.VMEM((nx, half, tall, LANES), BF16),
        pltpu.VMEM((ny * rows, LANES), BF16),
        pltpu.VMEM((half * rows, LANES), BF16),
        pltpu.VMEM((ny * rows, LANES), F32),
        pltpu.VMEM((ny * rows, LANES), F32),
        pltpu.VMEM((half * rows, LANES), F32),
        pltpu.VMEM((half, 2, 2 * block, LANES), BF16),
        pltpu.VMEM((ny, 2 * block, LANES), BF16),
        pltpu.VMEM((2 * block, ny * HD), BF16),
        pltpu.VMEM((2, half * HD, model), BF16),
        pltpu.VMEM((model, 2, columns), BF16),
        pltpu.VMEM((model, 2 * columns), BF16),
        pltpu.VMEM((block, model), BF16),
        pltpu.VMEM((block, model), F32),
        pltpu.VMEM((block, model), BF16),
        pltpu.VMEM((block, model), BF16),
        pltpu.VMEM((4, block, model), BF16),
        pltpu.VMEM((2, rim, columns), BF16),
        pltpu.VMEM((2, rim, columns), BF16),
        dma((half,)),
        dma((half,)),
        dma((ny,)),
        dma((half,)),
        dma((nx, half)),
        dma((half,)),
        dma((half,)),
        dma((half,)),
        dma((half,)),
        dma((half,)),
        dma((half, 2)),
        dma((ny,)),
        dma,
        dma,
        dma((3,)),
        dma((pieces,)),
        dma((pieces,)),
        dma((pieces,)),
        dma((pieces,)),
        dma((pieces,)),
        dma((4, pieces)),
        dma((2,)),
        dma((2,)),
    ]
    attended, padded = pl.pallas_call(
        functools.partial(kernel, ny, nx),
        out_shape=(
            jax.ShapeDtypeStruct((block, model), BF16),
            jax.ShapeDtypeStruct((rows + 2 * rim, columns), F32),
        ),
        in_specs=[anywhere, vmem, vmem, vmem, anywhere, vmem, vmem, anywhere],
        out_specs=(vmem, vmem),
        scratch_shapes=scratch,
        compiler_params=pltpu.CompilerParams(
            collective_id=0, has_side_effects=True, vmem_limit_bytes=56 * 1024 * 1024
        ),
        cost_estimate=pl.CostEstimate(
            flops=3 * 10**9, bytes_accessed=10**7, transcendentals=5 * 10**6
        ),
    )(
        residual_in,
        queries,
        keys,
        values,
        out_weight,
        norm_gain,
        norm_bias,
        glu_weight,
    )
    return pl.pallas_call(
        convolve,
        out_shape=(
            jax.ShapeDtypeStruct((block, model), BF16),
            jax.ShapeDtypeStruct((rows, columns), BF16),
        ),
        in_specs=[vmem] * 5,
        out_specs=(vmem, vmem),
    )(attended, padded, conv_weight, conv_scale, conv_shift)


def solution(mesh):
    return jax.shard_map(
        functools.partial(shards, mesh.shape["ctx"]),
        mesh=mesh,
        in_specs=(
            P(("dp", "ctx"), None),
            P(("dp", "ctx"), "tp"),
            P(("dp", "ctx"), "tp"),
            P(("dp", "ctx"), "tp"),
            P("tp", None),
            P(),
            P(),
            P(None, None, "tp"),
            P(None, "tp"),
            P("tp"),
            P("tp"),
        ),
        out_specs=(P(("dp", "ctx", "tp"), None), P(("dp", "ctx"), "tp")),
        check_vma=False,
    )
```

```python
import functools
import math

import jax
import jax.numpy as jnp
from jax import lax
from jax.experimental import pallas as pl
from jax.experimental.pallas import tpu as pltpu
from jax.sharding import PartitionSpec as P

KERNEL = 31
HD = 96
LANES = 128
MESH = pl.DeviceIdType.MESH
F32 = jnp.float32
BF16 = jnp.bfloat16


def wait_for(ref, sem):
    pltpu.make_async_copy(ref, ref, sem).wait()


def send(src, dst, send_sem, recv_sem, device):
    pltpu.make_async_remote_copy(
        src_ref=src,
        dst_ref=dst,
        send_sem=send_sem,
        recv_sem=recv_sem,
        device_id=device,
        device_id_type=MESH,
    ).start()


def send_or_keep(here, src, dst, send_sem, recv_sem, device):
    @pl.when(here)
    def _():
        pltpu.make_async_copy(src, dst, recv_sem).start()

    @pl.when(jnp.logical_not(here))
    def _():
        send(src, dst, send_sem, recv_sem, device)


def kernel(
    ny,
    nx,
    resid_in,
    q_in,
    k_in,
    v_in,
    w_ref,
    gain_in,
    bias_in,
    glu_ref,
    att_ref,
    gpad,
    q_ref,
    k_ref,
    v_ref,
    gain_ref,
    bias_ref,
    qs,
    kvs,
    qbuf,
    kvbuf,
    qfull,
    vfull,
    top,
    acc,
    accr,
    ctxs,
    cbuf,
    cat,
    wall,
    graw,
    gw,
    resid,
    own,
    zs,
    zr,
    nbuf,
    hs,
    hr,
    sq_s,
    skv_s,
    q_r,
    qf_s,
    kv_r,
    xr_s,
    xl_s,
    xf_s,
    a_s,
    a_r,
    c_s,
    c_r,
    w_s,
    w_r,
    l_r,
    z_s,
    z_r,
    nz_s,
    ns_s,
    nf_s,
    n_r,
    h_s,
    h_r,
):
    half = ny // 2
    rows = q_in.shape[0]
    block = rows // 4
    rim = gpad.shape[0] - rows
    rim = rim // 2
    width = gpad.shape[1]
    dp = lax.axis_index("dp")
    ctx = lax.axis_index("ctx")
    tp = lax.axis_index("tp")
    n_ctx = ny * nx
    y, x = ctx // nx, ctx % nx
    zh, core = tp // 2, tp % 2
    parity = y % 2

    def dev(yy, xx, tt):
        return (dp, yy * nx + xx, tt)

    sibling = (dp, ctx, zh * 2 + 1 - core)
    partner = (dp, ctx, (1 - zh) * 2 + core)
    x_right, x_left, x_far = (x + 1) % nx, (x + nx - 1) % nx, (x + 2) % nx
    right, left = dev(y, x_right, tp), dev(y, x_left, tp)

    loads = [
        pltpu.make_async_copy(src, dst, l_r.at[i])
        for i, (src, dst) in enumerate(
            (
                (k_in, k_ref),
                (v_in, v_ref),
                (q_in, q_ref),
                (w_ref, wall.at[core]),
                (glu_ref, graw),
                (resid_in.at[pl.ds(pl.multiple_of(tp * block, block), block)], resid),
                (gain_in, gain_ref),
                (bias_in, bias_ref),
            )
        )
    ]
    load_k, load_v, load_q, own_w, own_g, own_x, load_gain, load_bias = loads
    for load in loads:
        load.start()
    barrier = pltpu.get_barrier_semaphore()

    def greet(device):
        pl.semaphore_signal(barrier, inc=1, device_id=device, device_id_type=MESH)

    for o in range(1, ny):
        for cc in range(2):
            greet(dev((y + o) % ny, x, zh * 2 + cc))
    greet(sibling)
    greet(partner)
    greet(right)
    greet(left)
    greet((dp, (ctx + 1) % n_ctx, tp))
    greet((dp, (ctx + n_ctx - 1) % n_ctx, tp))

    cut = rows * 3 // 4
    part = rows - cut
    load_k.wait()
    load_v.wait()
    for j in range(half):
        lo = HD * j
        kvs[j, 0:rows] = jnp.concatenate(
            [k_ref[:, lo : lo + HD], v_ref[:, lo : lo + 32]], axis=1
        )
        kvs[j, rows : rows + rows // 2] = jnp.concatenate(
            [v_ref[0 : rows // 2, lo + 32 : lo + HD], v_ref[rows // 2 : rows, lo + 32 : lo + HD]],
            axis=1,
        )

    pl.semaphore_wait(barrier, 2 * (ny - 1) + 6)

    def rank(distance):
        sign = distance // (half + 1)
        fold = distance + sign * (ny - 2 * distance)
        odd = distance % 2
        return odd * (fold // 2 * 2 + sign) + (1 - odd) * (fold // 2 + fold // half + sign)

    near = [0]
    for o in range(1, half):
        near += [o, ny - o]
    near.append(half)

    def to_head(o, src, dst, send_sem, recv_sem):
        head = (y + o) % ny
        j = head % half
        device = dev(head, x, zh * 2 + parity)

        @pl.when(head // half == core)
        def _():
            if o == 0:
                send_or_keep(core == parity, src.at[j], dst, send_sem.at[j], recv_sem, device)
            else:
                send(src.at[j], dst, send_sem.at[j], recv_sem, device)

    def kv_to_head(o):
        place = rank((ny - o) % ny)
        to_head(o, kvs, kvbuf.at[x, place], skv_s, kv_r.at[x, place])

    for o in near[:3]:
        kv_to_head(o)
    load_q.wait()
    for j in range(half):
        lo = HD * j
        qs[j] = jnp.concatenate(
            [
                q_ref[0:cut, lo : lo + HD],
                jnp.concatenate(
                    [q_ref[cut:rows, lo + 32 * i : lo + 32 * (i + 1)] for i in range(3)], axis=0
                ),
            ],
            axis=1,
        )
    for o in near[::-1]:
        to_head(o, qs, qbuf.at[y], sq_s, q_r.at[y])
    for o in near[3:]:
        kv_to_head(o)

    def spread(s):
        wait_for(kvbuf.at[x, s], kv_r.at[x, s])
        send(kvbuf.at[x, s], kvbuf.at[x, s], xr_s.at[s], kv_r.at[x, s], right)
        send(kvbuf.at[x, s], kvbuf.at[x, s], xl_s.at[s], kv_r.at[x, s], left)

    def pass_on(s):
        slot, target = (x_left, right) if s % 2 == 0 else (x_right, left)
        wait_for(kvbuf.at[slot, s], kv_r.at[slot, s])
        send(kvbuf.at[slot, s], kvbuf.at[slot, s], xf_s.at[s], kv_r.at[slot, s], target)

    def arrive(slot, s):
        wait_for(kvbuf.at[slot, s], kv_r.at[slot, s])

    span = graw.shape[0] // half

    def relayout(i):
        @pl.loop(0, span // 16)
        def _(r):
            at = pl.ds(pl.multiple_of(i * span + r * 16, 16), 16)
            pair = graw[at].astype(F32)
            gw[at] = jnp.concatenate([pair[:, 0, :], pair[:, 1, :]], axis=1).astype(BF16)

    spread(0)
    for i in range(half):
        ys = 2 * ((y // 2 + i + 1) % half) + core
        wait_for(qbuf.at[ys], q_r.at[ys])
        send(qbuf.at[ys], qbuf.at[ys], qf_s.at[i], q_r.at[ys], sibling)
    own_g.wait()
    relayout(0)
    spread(1)
    send(w_ref, wall.at[core], w_s, w_r, sibling)
    relayout(1)
    pass_on(0)
    for i in range(half):
        ys = 2 * ((y // 2 + i) % half) + 1 - core
        wait_for(qbuf.at[ys], q_r.at[ys])

    @pl.loop(0, ny)
    def _(t):
        base = pl.multiple_of(t * rows, rows)
        qfull[pl.ds(base, cut)] = jnp.concatenate(
            [qbuf[t, :, 0:HD], jnp.zeros((cut, LANES - HD), BF16)], axis=1
        )
        qfull[pl.ds(base + cut, part)] = jnp.concatenate(
            [qbuf[t, part * i : part * (i + 1), HD:LANES] for i in range(3)]
            + [jnp.zeros((part, LANES - HD), BF16)],
            axis=1,
        )

    pass_on(1)
    relayout(2)
    factor = math.log2(math.e) / math.sqrt(HD)
    hr_rows = rows // 2
    tall = rows + hr_rows

    quarter = half // 2

    def unpack(slots, first_place):
        ones = jnp.ones((hr_rows, LANES - HD), BF16)
        for n, slot in enumerate(slots):
            for m in range(quarter):
                for b in range(2):
                    base = (n * quarter + m) * rows + b * hr_rows
                    vfull[base : base + hr_rows] = jnp.concatenate(
                        [
                            kvbuf[slot, first_place + m, b * hr_rows : (b + 1) * hr_rows, HD:LANES],
                            kvbuf[slot, first_place + m, rows:tall, 64 * b : 64 * (b + 1)],
                            ones,
                        ],
                        axis=1,
                    )

    wide = 2 * rows

    def tile(slots, place, base, first):
        at = pl.ds(pl.multiple_of(base, wide), wide)
        kk = jnp.concatenate(
            [
                kvbuf[slot, place : place + quarter, 0:rows, :].reshape(quarter * rows, LANES)
                for slot in slots
            ],
            axis=0,
        )
        s = lax.dot_general(
            qfull[at], kk, (((1,), (1,)), ((), ())), preferred_element_type=F32
        )
        peak = jnp.max(s, axis=1, keepdims=True) * factor
        if first:
            new = peak
        else:
            old = top[at][:, 0:1]
            new = jnp.maximum(old, peak)
        p = jnp.exp2(s * factor - new)
        mix = jnp.dot(p.astype(BF16), vfull[...], preferred_element_type=F32)
        if not first:
            mix = mix + acc[at] * jnp.exp2(old - new)
        return at, mix, new

    def attend(slots, place, first):
        unpack(slots, place)
        for t in range(half):
            at, mix, new = tile(slots, place, t * wide, first)
            acc[at] = mix
            top[at] = jnp.broadcast_to(new, (wide, LANES))

    arrive(x_left, 1)
    attend((x, x_left), 0, True)
    spread(2)
    relayout(3)
    spread(3)
    arrive(x_right, 0)
    arrive(x_far, 0)
    arrive(x_far, 1)
    attend((x_right, x_far), 0, False)
    pass_on(2)
    pass_on(3)
    arrive(x_left, 3)
    attend((x, x_left), 2, False)
    arrive(x_right, 2)
    arrive(x_far, 2)
    arrive(x_far, 3)
    last = (x_right, x_far)
    unpack(last, 2)
    lane = lax.broadcasted_iota(jnp.int32, (wide, LANES), 1)
    for t in range(half // 2):
        at, mix, new = tile(last, 2, (1 - core) * half * rows + t * wide, False)
        acc[at] = jnp.where(lane >= LANES - 16, jnp.broadcast_to(new, (wide, LANES)), mix)
        send(acc.at[at], accr.at[pl.ds(t * wide, wide)], a_s.at[t], a_r.at[t], sibling)
    for t in range(half // 2):
        at, mix, new = tile(last, 2, core * half * rows + t * wide, False)
        acc[at] = mix
        top[at] = jnp.broadcast_to(new, (wide, LANES))
    for t in range(half // 2):
        wait_for(accr.at[pl.ds(t * wide, wide)], a_r.at[t])
        for k in range(2 * t, 2 * t + 2):
            yd = core * half + k
            at = pl.ds(pl.multiple_of(yd * rows, rows), rows)
            other = accr[k * rows : (k + 1) * rows]
            other_top = other[:, LANES - 1 : LANES]
            new = top[at][:, 0:1]
            both = jnp.maximum(new, other_top)
            total = acc[at] * jnp.exp2(new - both) + other * jnp.exp2(other_top - both)
            out = (total / total[:, HD : HD + 1]).astype(BF16)
            for cc in range(2):
                for zz in range(2):
                    src = (zz * 2 + cc) * block
                    ctxs[k, cc, zz * block : (zz + 1) * block] = out[src : src + block]
            for cc in range(2):
                send_or_keep(
                    jnp.logical_and(yd == y, core == cc),
                    ctxs.at[k, cc],
                    cbuf.at[y],
                    c_s.at[k, cc],
                    c_r.at[y],
                    dev(yd, x, zh * 2 + cc),
                )

    for load in (own_w, own_x, load_gain, load_bias):
        load.wait()
    wait_for(wall.at[1 - core], w_r)
    for h in range(ny):
        wait_for(cbuf.at[h], c_r.at[h])
        cat[:, HD * h : HD * (h + 1)] = cbuf[h, :, 0:HD]

    def project(zz):
        return jnp.dot(
            cat[pl.ds(pl.multiple_of(zz * block, block), block)],
            wall[...].reshape(wall.shape[0] * wall.shape[1], wall.shape[2]),
            preferred_element_type=F32,
        )

    pieces = z_s.shape[0]
    step = block // pieces
    zs[...] = project(1 - zh).astype(BF16)
    for i in range(pieces):
        send(
            zs.at[pl.ds(i * step, step)],
            zr.at[pl.ds(i * step, step)],
            z_s.at[i],
            z_r.at[i],
            partner,
        )
    own[...] = project(zh) + resid[...].astype(F32)
    for i in range(pieces):
        piece = pl.ds(i * step, step)
        wait_for(zr.at[piece], z_r.at[i])
        attended = (own[piece] + zr[piece].astype(F32)).astype(BF16)
        att_ref[piece] = attended
        full = attended.astype(F32)
        centred = full - jnp.mean(full, axis=1, keepdims=True)
        var = jnp.mean(centred * centred, axis=1, keepdims=True)
        normed = centred * lax.rsqrt(var + 1e-05) * gain_ref[...].reshape(1, -1)
        nbuf[tp, piece] = (normed + bias_ref[...].reshape(1, -1)).astype(BF16)
        send(nbuf.at[tp, piece], nbuf.at[tp, piece], nz_s.at[i], n_r.at[tp, i], partner)
        send(nbuf.at[tp, piece], nbuf.at[tp, piece], ns_s.at[i], n_r.at[tp, i], sibling)

    def gate(zz):
        data = nbuf[pl.ds(zz * 2, 2)].reshape(2 * block, nbuf.shape[2])
        projected = jnp.dot(data, gw[...], preferred_element_type=F32)
        gated = projected[:, 0:width] * jax.nn.sigmoid(projected[:, width:])
        base = pl.multiple_of(rim + zz * 2 * block, 16)
        gpad[pl.ds(base, 2 * block)] = gated.astype(BF16).astype(F32)
        edge = pl.multiple_of(rim + zz * (rows - rim), 16)
        hs[zz] = gpad[pl.ds(edge, rim)].astype(BF16)
        target = ctx + 2 * zz - 1

        @pl.when(jnp.logical_and(target >= 0, target < n_ctx))
        def _():
            send(hs.at[zz], hr.at[1 - zz], h_s.at[zz], h_r.at[1 - zz], (dp, target, tp))

    for i in range(pieces):
        wait_for(
            nbuf.at[zh * 2 + 1 - core, pl.ds(i * step, step)], n_r.at[zh * 2 + 1 - core, i]
        )
    gate(zh)
    tp_other = (1 - zh) * 2 + core
    for i in range(pieces):
        piece = pl.ds(i * step, step)
        wait_for(nbuf.at[tp_other, piece], n_r.at[tp_other, i])
        send(
            nbuf.at[tp_other, piece],
            nbuf.at[tp_other, piece],
            nf_s.at[i],
            n_r.at[tp_other, i],
            sibling,
        )
    for i in range(pieces):
        tp_last = (1 - zh) * 2 + 1 - core
        wait_for(nbuf.at[tp_last, pl.ds(i * step, step)], n_r.at[tp_last, i])
    gate(1 - zh)

    for side in range(2):
        source = ctx + 2 * side - 1
        exists = jnp.logical_and(source >= 0, source < n_ctx)
        place = pl.ds(side * (rim + rows), rim)

        @pl.when(exists)
        def _():
            wait_for(hr.at[side], h_r.at[side])
            gpad[place] = hr[side].astype(F32)

        @pl.when(jnp.logical_not(exists))
        def _():
            gpad[place] = jnp.zeros((rim, width), F32)

    for j in range(half):
        here = jnp.logical_and(core * half + j == y, core == parity)

        @pl.when(jnp.logical_not(here))
        def _():
            wait_for(qs.at[j], sq_s.at[j])
            wait_for(kvs.at[j], skv_s.at[j])

        wait_for(qbuf.at[j], qf_s.at[j])
        wait_for(kvbuf.at[x, j], xr_s.at[j])
        wait_for(kvbuf.at[x, j], xl_s.at[j])
        wait_for(kvbuf.at[x, j], xf_s.at[j])
        for cc in range(2):

            @pl.when(jnp.logical_not(jnp.logical_and(core * half + j == y, core == cc)))
            def _():
                wait_for(ctxs.at[j, cc], c_s.at[j, cc])

    wait_for(wall.at[core], w_s)
    for t in range(half // 2):
        wait_for(accr.at[pl.ds(t * wide, wide)], a_s.at[t])
    for i in range(pieces):
        piece = pl.ds(i * step, step)
        wait_for(zs.at[piece], z_s.at[i])
        wait_for(nbuf.at[tp, piece], nz_s.at[i])
        wait_for(nbuf.at[tp, piece], ns_s.at[i])
        wait_for(nbuf.at[tp_other, piece], nf_s.at[i])
    for side in range(2):
        target = ctx + 2 * side - 1

        @pl.when(jnp.logical_and(target >= 0, target < n_ctx))
        def _():
            wait_for(hs.at[side], h_s.at[side])


def convolve(att_in, gpad, taps_ref, scale_ref, shift_ref, att_ref, conv_ref):
    rows = conv_ref.shape[0]
    rim = (gpad.shape[0] - rows) // 2
    att_ref[...] = att_in[...]
    offset = rim - (KERNEL - 1) // 2
    taps = taps_ref[...]
    scale = scale_ref[...].reshape(1, -1)
    shift = shift_ref[...].reshape(1, -1)

    for r in range(0, rows, 4 * rim):
        for lane in range(0, conv_ref.shape[1], LANES):
            at = slice(lane, lane + LANES)
            window = gpad[r : r + 6 * rim, at]
            total = None
            for turn in range(8):
                places = [p for p in range(offset, offset + KERNEL) if p % 8 == turn]
                top = places[-1] + 4 * rim
                turned = window[turn : turn + (top - turn) // 8 * 8]
                for p in places:
                    term = turned[p - turn : p - turn + 4 * rim] * taps[p - offset : p - offset + 1, at]
                    total = term if total is None else total + term
            u = total * scale[:, at] + shift[:, at]
            conv_ref[r : r + 4 * rim, at] = (u * jax.nn.sigmoid(u)).astype(BF16)


def shards(
    n_ctx,
    residual_in,
    queries,
    keys,
    values,
    out_weight,
    norm_gain,
    norm_bias,
    glu_weight,
    conv_weight,
    conv_scale,
    conv_shift,
):
    rows, columns = queries.shape
    half = columns // HD
    ny = 2 * half
    nx = n_ctx // ny
    model = residual_in.shape[1]
    block = rows // 4
    pieces = block // 16
    rim = 16
    vmem = pl.BlockSpec(memory_space=pltpu.VMEM)
    anywhere = pl.BlockSpec(memory_space=pl.ANY)
    dma = pltpu.SemaphoreType.DMA
    tall = rows + rows // 2
    scratch = [
        pltpu.VMEM((rows, columns), BF16),
        pltpu.VMEM((rows, columns), BF16),
        pltpu.VMEM((rows, columns), BF16),
        pltpu.VMEM((model,), F32),
        pltpu.VMEM((model,), F32),
        pltpu.VMEM((half, rows * 3 // 4, LANES), BF16),
        pltpu.VMEM((half, tall, LANES), BF16),
        pltpu.VMEM((ny, rows * 3 // 4, LANES), BF16),
        pltpu.VMEM((nx, half, tall, LANES), BF16),
        pltpu.VMEM((ny * rows, LANES), BF16),
        pltpu.VMEM((half * rows, LANES), BF16),
        pltpu.VMEM((ny * rows, LANES), F32),
        pltpu.VMEM((ny * rows, LANES), F32),
        pltpu.VMEM((half * rows, LANES), F32),
        pltpu.VMEM((half, 2, 2 * block, LANES), BF16),
        pltpu.VMEM((ny, 2 * block, LANES), BF16),
        pltpu.VMEM((2 * block, ny * HD), BF16),
        pltpu.VMEM((2, half * HD, model), BF16),
        pltpu.VMEM((model, 2, columns), BF16),
        pltpu.VMEM((model, 2 * columns), BF16),
        pltpu.VMEM((block, model), BF16),
        pltpu.VMEM((block, model), F32),
        pltpu.VMEM((block, model), BF16),
        pltpu.VMEM((block, model), BF16),
        pltpu.VMEM((4, block, model), BF16),
        pltpu.VMEM((2, rim, columns), BF16),
        pltpu.VMEM((2, rim, columns), BF16),
        dma((half,)),
        dma((half,)),
        dma((ny,)),
        dma((half,)),
        dma((nx, half)),
        dma((half,)),
        dma((half,)),
        dma((half,)),
        dma((half,)),
        dma((half,)),
        dma((half, 2)),
        dma((ny,)),
        dma,
        dma,
        dma((8,)),
        dma((pieces,)),
        dma((pieces,)),
        dma((pieces,)),
        dma((pieces,)),
        dma((pieces,)),
        dma((4, pieces)),
        dma((2,)),
        dma((2,)),
    ]
    attended, padded = pl.pallas_call(
        functools.partial(kernel, ny, nx),
        out_shape=(
            jax.ShapeDtypeStruct((block, model), BF16),
            jax.ShapeDtypeStruct((rows + 2 * rim, columns), F32),
        ),
        in_specs=[anywhere] * 8,
        out_specs=(vmem, vmem),
        scratch_shapes=scratch,
        compiler_params=pltpu.CompilerParams(
            collective_id=0, has_side_effects=True, vmem_limit_bytes=56 * 1024 * 1024
        ),
        cost_estimate=pl.CostEstimate(
            flops=3 * 10**9, bytes_accessed=10**7, transcendentals=5 * 10**6
        ),
    )(
        residual_in,
        queries,
        keys,
        values,
        out_weight,
        norm_gain,
        norm_bias,
        glu_weight,
    )
    return pl.pallas_call(
        convolve,
        out_shape=(
            jax.ShapeDtypeStruct((block, model), BF16),
            jax.ShapeDtypeStruct((rows, columns), BF16),
        ),
        in_specs=[vmem] * 5,
        out_specs=(vmem, vmem),
    )(attended, padded, conv_weight, conv_scale, conv_shift)


def solution(mesh):
    return jax.shard_map(
        functools.partial(shards, mesh.shape["ctx"]),
        mesh=mesh,
        in_specs=(
            P(("dp", "ctx"), None),
            P(("dp", "ctx"), "tp"),
            P(("dp", "ctx"), "tp"),
            P(("dp", "ctx"), "tp"),
            P("tp", None),
            P(),
            P(),
            P(None, None, "tp"),
            P(None, "tp"),
            P("tp"),
            P("tp"),
        ),
        out_specs=(P(("dp", "ctx", "tp"), None), P(("dp", "ctx"), "tp")),
        check_vma=False,
    )
```

```python
import functools
import math

import jax
import jax.numpy as jnp
from jax import lax
from jax.experimental import pallas as pl
from jax.experimental.pallas import tpu as pltpu
from jax.sharding import PartitionSpec as P

KERNEL = 31
HD = 96
LANES = 128
MESH = pl.DeviceIdType.MESH
F32 = jnp.float32
BF16 = jnp.bfloat16


def wait_for(ref, sem):
    pltpu.make_async_copy(ref, ref, sem).wait()


def send(src, dst, send_sem, recv_sem, device):
    pltpu.make_async_remote_copy(
        src_ref=src,
        dst_ref=dst,
        send_sem=send_sem,
        recv_sem=recv_sem,
        device_id=device,
        device_id_type=MESH,
    ).start()


def send_or_keep(here, src, dst, send_sem, recv_sem, device):
    @pl.when(here)
    def _():
        pltpu.make_async_copy(src, dst, recv_sem).start()

    @pl.when(jnp.logical_not(here))
    def _():
        send(src, dst, send_sem, recv_sem, device)


def kernel(
    ny,
    nx,
    resid_in,
    q_in,
    k_in,
    v_in,
    w_ref,
    gain_in,
    bias_in,
    glu_ref,
    att_ref,
    gpad,
    q_ref,
    k_ref,
    v_ref,
    gain_ref,
    bias_ref,
    qs,
    kvs,
    qbuf,
    kvbuf,
    qfull,
    vfull,
    top,
    acc,
    accr,
    ctxs,
    cbuf,
    cat,
    wall,
    graw,
    gw,
    resid,
    nbuf,
    hs,
    hr,
    sq_s,
    skv_s,
    q_r,
    qf_s,
    kv_r,
    xr_s,
    xl_s,
    xf_s,
    a_s,
    a_r,
    c_s,
    c_r,
    w_s,
    w_r,
    l_r,
    z_s,
    z_r,
    n_s,
    n_r,
    wa_s,
    wa_r,
    wb_s,
    wb_r,
    wf_s,
    wf_r,
    h_s,
    h_r,
):
    half = ny // 2
    rows = q_in.shape[0]
    block = rows // 4
    rim = gpad.shape[0] - rows
    rim = rim // 2
    width = gpad.shape[1]
    dp = lax.axis_index("dp")
    ctx = lax.axis_index("ctx")
    tp = lax.axis_index("tp")
    n_ctx = ny * nx
    y, x = ctx // nx, ctx % nx
    zh, core = tp // 2, tp % 2
    parity = y % 2

    def dev(yy, xx, tt):
        return (dp, yy * nx + xx, tt)

    sibling = (dp, ctx, zh * 2 + 1 - core)
    away, away_sibling = (1 - zh) * 2 + core, (1 - zh) * 2 + 1 - core
    partner = (dp, ctx, away)
    n_dp = lax.axis_size("dp")
    above = (zh * n_dp + dp + 1) % (2 * n_dp)
    below = (zh * n_dp + dp + 2 * n_dp - 1) % (2 * n_dp)
    up = (above % n_dp, ctx, above // n_dp * 2 + core)
    down = (below % n_dp, ctx, below // n_dp * 2 + core)
    x_right, x_left, x_far = (x + 1) % nx, (x + nx - 1) % nx, (x + 2) % nx
    right, left = dev(y, x_right, tp), dev(y, x_left, tp)

    loads = [
        pltpu.make_async_copy(src, dst, l_r.at[i])
        for i, (src, dst) in enumerate(
            (
                (k_in, k_ref),
                (v_in, v_ref),
                (q_in, q_ref),
                (w_ref, wall.at[tp]),
                (glu_ref, graw),
                (resid_in.at[pl.ds(pl.multiple_of(core * block, block), block)], resid.at[0:block]),
                (
                    resid_in.at[pl.ds(pl.multiple_of((2 + core) * block, block), block)],
                    resid.at[block : 2 * block],
                ),
                (gain_in, gain_ref),
                (bias_in, bias_ref),
            )
        )
    ]
    load_k, load_v, load_q, own_w, own_g, own_x, own_x2, load_gain, load_bias = loads
    for load in loads:
        load.start()
    barrier = pltpu.get_barrier_semaphore()

    def greet(device):
        pl.semaphore_signal(barrier, inc=1, device_id=device, device_id_type=MESH)

    for o in range(1, ny):
        for cc in range(2):
            greet(dev((y + o) % ny, x, zh * 2 + cc))
    greet(sibling)
    greet(partner)
    greet(up)
    greet(down)
    greet(right)
    greet(left)
    greet((dp, (ctx + 1) % n_ctx, tp))
    greet((dp, (ctx + n_ctx - 1) % n_ctx, tp))

    cut = rows * 3 // 4
    part = rows - cut
    load_k.wait()
    load_v.wait()
    for j in range(half):
        lo = HD * j
        kvs[j, 0:rows] = jnp.concatenate(
            [k_ref[:, lo : lo + HD], v_ref[:, lo : lo + 32]], axis=1
        )
        kvs[j, rows : rows + rows // 2] = jnp.concatenate(
            [v_ref[0 : rows // 2, lo + 32 : lo + HD], v_ref[rows // 2 : rows, lo + 32 : lo + HD]],
            axis=1,
        )

    pl.semaphore_wait(barrier, 2 * (ny - 1) + 8)

    def rank(distance):
        sign = distance // (half + 1)
        fold = distance + sign * (ny - 2 * distance)
        odd = distance % 2
        return odd * (fold // 2 * 2 + sign) + (1 - odd) * (fold // 2 + fold // half + sign)

    near = [0]
    for o in range(1, half):
        near += [o, ny - o]
    near.append(half)

    def to_head(o, src, dst, send_sem, recv_sem):
        head = (y + o) % ny
        j = head % half
        device = dev(head, x, zh * 2 + parity)

        @pl.when(head // half == core)
        def _():
            if o == 0:
                send_or_keep(core == parity, src.at[j], dst, send_sem.at[j], recv_sem, device)
            else:
                send(src.at[j], dst, send_sem.at[j], recv_sem, device)

    def kv_to_head(o):
        place = rank((ny - o) % ny)
        to_head(o, kvs, kvbuf.at[x, place], skv_s, kv_r.at[x, place])

    for o in near[:3]:
        kv_to_head(o)
    pieces = wa_s.shape[0]
    piece_rows = w_ref.shape[0] // (2 * pieces)

    def piece_of(ref, side, i):
        start = side * (w_ref.shape[0] // 2) + i * piece_rows
        return ref.at[pl.ds(pl.multiple_of(start, 16), piece_rows)]

    @pl.when(dp == 0)
    def _():
        for i in range(pieces):
            src, dst = piece_of(w_ref, 0, i), piece_of(wall.at[tp], 0, i)
            send(src, dst, wa_s.at[i], wa_r.at[i], down)

    @pl.when(dp == n_dp - 1)
    def _():
        for i in range(pieces):
            src, dst = piece_of(w_ref, 1, i), piece_of(wall.at[tp], 1, i)
            send(src, dst, wb_s.at[i], wb_r.at[i], up)

    def relay(slot):
        for side, hop, s_sem, r_sem, target in (
            (0, n_dp - 1 - dp, wa_s, wa_r, down),
            (1, dp, wb_s, wb_r, up),
        ):
            i = slot - hop

            @pl.when(jnp.logical_and(i >= 0, i < pieces))
            def _():
                held = piece_of(wall.at[away], side, i)
                wait_for(held, r_sem.at[i])

                @pl.when(hop < n_dp - 1)
                def _():
                    send(held, held, s_sem.at[i], r_sem.at[i], target)

                send(held, held, wf_s.at[side, i], wf_r.at[side, i], sibling)

    load_q.wait()
    for j in range(half):
        lo = HD * j
        qs[j] = jnp.concatenate(
            [
                q_ref[0:cut, lo : lo + HD],
                jnp.concatenate(
                    [q_ref[cut:rows, lo + 32 * i : lo + 32 * (i + 1)] for i in range(3)], axis=0
                ),
            ],
            axis=1,
        )
    for o in near[::-1]:
        to_head(o, qs, qbuf.at[y], sq_s, q_r.at[y])
    for o in near[3:]:
        kv_to_head(o)

    def spread(s):
        wait_for(kvbuf.at[x, s], kv_r.at[x, s])
        send(kvbuf.at[x, s], kvbuf.at[x, s], xr_s.at[s], kv_r.at[x, s], right)
        send(kvbuf.at[x, s], kvbuf.at[x, s], xl_s.at[s], kv_r.at[x, s], left)

    def pass_on(s):
        slot, target = (x_left, right) if s % 2 == 0 else (x_right, left)
        wait_for(kvbuf.at[slot, s], kv_r.at[slot, s])
        send(kvbuf.at[slot, s], kvbuf.at[slot, s], xf_s.at[s], kv_r.at[slot, s], target)

    def arrive(slot, s):
        wait_for(kvbuf.at[slot, s], kv_r.at[slot, s])

    span = graw.shape[0] // half

    def relayout(i):
        @pl.loop(0, span // 16)
        def _(r):
            at = pl.ds(pl.multiple_of(i * span + r * 16, 16), 16)
            pair = graw[at].astype(F32)
            gw[at] = jnp.concatenate([pair[:, 0, :], pair[:, 1, :]], axis=1).astype(BF16)

    spread(0)
    for i in range(half):
        ys = 2 * ((y // 2 + i + 1) % half) + core
        wait_for(qbuf.at[ys], q_r.at[ys])
        send(qbuf.at[ys], qbuf.at[ys], qf_s.at[i], q_r.at[ys], sibling)
    relay(0)
    own_g.wait()
    relayout(0)
    spread(1)
    send(w_ref, wall.at[tp], w_s, w_r, sibling)
    relay(1)
    relayout(1)
    pass_on(0)
    for i in range(half):
        ys = 2 * ((y // 2 + i) % half) + 1 - core
        wait_for(qbuf.at[ys], q_r.at[ys])

    @pl.loop(0, ny)
    def _(t):
        base = pl.multiple_of(t * rows, rows)
        qfull[pl.ds(base, cut)] = jnp.concatenate(
            [qbuf[t, :, 0:HD], jnp.zeros((cut, LANES - HD), BF16)], axis=1
        )
        qfull[pl.ds(base + cut, part)] = jnp.concatenate(
            [qbuf[t, part * i : part * (i + 1), HD:LANES] for i in range(3)]
            + [jnp.zeros((part, LANES - HD), BF16)],
            axis=1,
        )

    pass_on(1)
    relay(2)
    relayout(2)
    factor = math.log2(math.e) / math.sqrt(HD)
    hr_rows = rows // 2
    tall = rows + hr_rows

    quarter = half // 2

    def unpack(slots, first_place):
        ones = jnp.ones((hr_rows, LANES - HD), BF16)
        for n, slot in enumerate(slots):
            for m in range(quarter):
                for b in range(2):
                    base = (n * quarter + m) * rows + b * hr_rows
                    vfull[base : base + hr_rows] = jnp.concatenate(
                        [
                            kvbuf[slot, first_place + m, b * hr_rows : (b + 1) * hr_rows, HD:LANES],
                            kvbuf[slot, first_place + m, rows:tall, 64 * b : 64 * (b + 1)],
                            ones,
                        ],
                        axis=1,
                    )

    wide = 2 * rows

    def tile(slots, place, base, first):
        at = pl.ds(pl.multiple_of(base, wide), wide)
        kk = jnp.concatenate(
            [
                kvbuf[slot, place : place + quarter, 0:rows, :].reshape(quarter * rows, LANES)
                for slot in slots
            ],
            axis=0,
        )
        s = lax.dot_general(
            qfull[at], kk, (((1,), (1,)), ((), ())), preferred_element_type=F32
        )
        peak = jnp.max(s, axis=1, keepdims=True) * factor
        if first:
            new = peak
        else:
            old = top[at][:, 0:1]
            new = jnp.maximum(old, peak)
        p = jnp.exp2(s * factor - new)
        mix = jnp.dot(p.astype(BF16), vfull[...], preferred_element_type=F32)
        if not first:
            mix = mix + acc[at] * jnp.exp2(old - new)
        return at, mix, new

    def attend(slots, place, first):
        unpack(slots, place)
        for t in range(half):
            at, mix, new = tile(slots, place, t * wide, first)
            acc[at] = mix
            top[at] = jnp.broadcast_to(new, (wide, LANES))

    arrive(x_left, 1)
    attend((x, x_left), 0, True)
    relay(3)
    spread(2)
    relayout(3)
    spread(3)
    relay(4)
    arrive(x_right, 0)
    arrive(x_far, 0)
    arrive(x_far, 1)
    attend((x_right, x_far), 0, False)
    pass_on(2)
    pass_on(3)
    relay(5)
    arrive(x_left, 3)
    attend((x, x_left), 2, False)
    relay(6)
    arrive(x_right, 2)
    arrive(x_far, 2)
    arrive(x_far, 3)
    last = (x_right, x_far)
    unpack(last, 2)
    lane = lax.broadcasted_iota(jnp.int32, (wide, LANES), 1)
    for t in range(half // 2):
        at, mix, new = tile(last, 2, (1 - core) * half * rows + t * wide, False)
        acc[at] = jnp.where(lane >= LANES - 16, jnp.broadcast_to(new, (wide, LANES)), mix)
        send(acc.at[at], accr.at[pl.ds(t * wide, wide)], a_s.at[t], a_r.at[t], sibling)
    relay(7)
    for t in range(half // 2):
        at, mix, new = tile(last, 2, core * half * rows + t * wide, False)
        acc[at] = mix
        top[at] = jnp.broadcast_to(new, (wide, LANES))
    for t in range(half // 2):
        wait_for(accr.at[pl.ds(t * wide, wide)], a_r.at[t])
        for k in range(2 * t, 2 * t + 2):
            yd = core * half + k
            at = pl.ds(pl.multiple_of(yd * rows, rows), rows)
            other = accr[k * rows : (k + 1) * rows]
            other_top = other[:, LANES - 1 : LANES]
            new = top[at][:, 0:1]
            both = jnp.maximum(new, other_top)
            total = acc[at] * jnp.exp2(new - both) + other * jnp.exp2(other_top - both)
            out = (total / total[:, HD : HD + 1]).astype(BF16)
            for cc in range(2):
                for zz in range(2):
                    src = (zz * 2 + cc) * block
                    ctxs[k, cc, zz * block : (zz + 1) * block] = out[src : src + block]
            for cc in range(2):
                send_or_keep(
                    jnp.logical_and(yd == y, core == cc),
                    ctxs.at[k, cc],
                    cbuf.at[y],
                    c_s.at[k, cc],
                    c_r.at[y],
                    dev(yd, x, zh * 2 + cc),
                )

    for slot in range(n_dp + 4, n_dp + pieces - 1):
        relay(slot)
    for load in (own_w, own_x, own_x2, load_gain, load_bias):
        load.wait()
    wait_for(wall.at[zh * 2 + 1 - core], w_r)
    total = resid[...].astype(F32)
    for g in range(2):
        for j in range(half):
            wait_for(cbuf.at[g * half + j], c_r.at[g * half + j])
            cat[zh, g, :, HD * j : HD * (j + 1)] = cbuf[g * half + j, :, 0:HD]
        send(cat.at[zh, g], cat.at[zh, g], z_s.at[g], z_r.at[g], partner)
    for g in range(2):
        total += jnp.dot(cat[zh, g], wall[zh * 2 + g], preferred_element_type=F32)
    for side in range(2):
        for i in range(pieces):
            wait_for(piece_of(wall.at[away_sibling], side, i), wf_r.at[side, i])
    for g in range(2):
        wait_for(cat.at[1 - zh, g], z_r.at[g])
        total += jnp.dot(cat[1 - zh, g], wall[(1 - zh) * 2 + g], preferred_element_type=F32)
    attended = total.astype(BF16)
    resid[...] = attended
    att_ref[...] = resid[pl.ds(pl.multiple_of(zh * block, block), block)]
    full = attended.astype(F32)
    centred = full - jnp.mean(full, axis=1, keepdims=True)
    var = jnp.mean(centred * centred, axis=1, keepdims=True)
    normed = centred * lax.rsqrt(var + 1e-05) * gain_ref[...].reshape(1, -1)
    nbuf[core] = (normed + bias_ref[...].reshape(1, -1)).astype(BF16)
    send(nbuf.at[core], nbuf.at[core], n_s, n_r, sibling)

    def gate(cc):
        projected = jnp.dot(nbuf[cc], gw[...], preferred_element_type=F32)
        gated = projected[:, 0:width] * jax.nn.sigmoid(projected[:, width:])
        gated = gated.astype(BF16).astype(F32)
        for zz in range(2):
            base = pl.multiple_of(rim + (zz * 2 + cc) * block, 16)
            gpad[pl.ds(base, block)] = gated[zz * block : (zz + 1) * block]
        edge = pl.multiple_of(rim + cc * (rows - rim), 16)
        hs[cc] = gpad[pl.ds(edge, rim)].astype(BF16)
        target = ctx + 2 * cc - 1

        @pl.when(jnp.logical_and(target >= 0, target < n_ctx))
        def _():
            send(hs.at[cc], hr.at[1 - cc], h_s.at[cc], h_r.at[1 - cc], (dp, target, tp))

    gate(core)
    wait_for(nbuf.at[1 - core], n_r)
    gate(1 - core)

    for side in range(2):
        source = ctx + 2 * side - 1
        exists = jnp.logical_and(source >= 0, source < n_ctx)
        place = pl.ds(side * (rim + rows), rim)

        @pl.when(exists)
        def _():
            wait_for(hr.at[side], h_r.at[side])
            gpad[place] = hr[side].astype(F32)

        @pl.when(jnp.logical_not(exists))
        def _():
            gpad[place] = jnp.zeros((rim, width), F32)

    for j in range(half):
        here = jnp.logical_and(core * half + j == y, core == parity)

        @pl.when(jnp.logical_not(here))
        def _():
            wait_for(qs.at[j], sq_s.at[j])
            wait_for(kvs.at[j], skv_s.at[j])

        wait_for(qbuf.at[j], qf_s.at[j])
        wait_for(kvbuf.at[x, j], xr_s.at[j])
        wait_for(kvbuf.at[x, j], xl_s.at[j])
        wait_for(kvbuf.at[x, j], xf_s.at[j])
        for cc in range(2):

            @pl.when(jnp.logical_not(jnp.logical_and(core * half + j == y, core == cc)))
            def _():
                wait_for(ctxs.at[j, cc], c_s.at[j, cc])

    wait_for(wall.at[tp], w_s)
    for t in range(half // 2):
        wait_for(accr.at[pl.ds(t * wide, wide)], a_s.at[t])
    for i in range(pieces):
        wait_for(piece_of(w_ref, 0, i), wa_s.at[i])
        wait_for(piece_of(w_ref, 1, i), wb_s.at[i])
        for side in range(2):
            wait_for(piece_of(w_ref, side, i), wf_s.at[side, i])
    for g in range(2):
        wait_for(cat.at[zh, g], z_s.at[g])
    wait_for(nbuf.at[core], n_s)
    for side in range(2):
        target = ctx + 2 * side - 1

        @pl.when(jnp.logical_and(target >= 0, target < n_ctx))
        def _():
            wait_for(hs.at[side], h_s.at[side])


def convolve(att_in, gpad, taps_ref, scale_ref, shift_ref, att_ref, conv_ref):
    rows = conv_ref.shape[0]
    rim = (gpad.shape[0] - rows) // 2
    att_ref[...] = att_in[...]
    offset = rim - (KERNEL - 1) // 2
    taps = taps_ref[...]
    scale = scale_ref[...].reshape(1, -1)
    shift = shift_ref[...].reshape(1, -1)

    for r in range(0, rows, 4 * rim):
        for lane in range(0, conv_ref.shape[1], LANES):
            at = slice(lane, lane + LANES)
            window = gpad[r : r + 6 * rim, at]
            total = None
            for turn in range(8):
                places = [p for p in range(offset, offset + KERNEL) if p % 8 == turn]
                top = places[-1] + 4 * rim
                turned = window[turn : turn + (top - turn) // 8 * 8]
                for p in places:
                    term = turned[p - turn : p - turn + 4 * rim] * taps[p - offset : p - offset + 1, at]
                    total = term if total is None else total + term
            u = total * scale[:, at] + shift[:, at]
            conv_ref[r : r + 4 * rim, at] = (u * jax.nn.sigmoid(u)).astype(BF16)


def shards(
    n_ctx,
    residual_in,
    queries,
    keys,
    values,
    out_weight,
    norm_gain,
    norm_bias,
    glu_weight,
    conv_weight,
    conv_scale,
    conv_shift,
):
    rows, columns = queries.shape
    half = columns // HD
    ny = 2 * half
    nx = n_ctx // ny
    model = residual_in.shape[1]
    block = rows // 4
    pieces = columns // 64
    rim = 16
    vmem = pl.BlockSpec(memory_space=pltpu.VMEM)
    anywhere = pl.BlockSpec(memory_space=pl.ANY)
    dma = pltpu.SemaphoreType.DMA
    tall = rows + rows // 2
    scratch = [
        pltpu.VMEM((rows, columns), BF16),
        pltpu.VMEM((rows, columns), BF16),
        pltpu.VMEM((rows, columns), BF16),
        pltpu.VMEM((model,), F32),
        pltpu.VMEM((model,), F32),
        pltpu.VMEM((half, rows * 3 // 4, LANES), BF16),
        pltpu.VMEM((half, tall, LANES), BF16),
        pltpu.VMEM((ny, rows * 3 // 4, LANES), BF16),
        pltpu.VMEM((nx, half, tall, LANES), BF16),
        pltpu.VMEM((ny * rows, LANES), BF16),
        pltpu.VMEM((half * rows, LANES), BF16),
        pltpu.VMEM((ny * rows, LANES), F32),
        pltpu.VMEM((ny * rows, LANES), F32),
        pltpu.VMEM((half * rows, LANES), F32),
        pltpu.VMEM((half, 2, 2 * block, LANES), BF16),
        pltpu.VMEM((ny, 2 * block, LANES), BF16),
        pltpu.VMEM((2, 2, 2 * block, columns), BF16),
        pltpu.VMEM((4, columns, model), BF16),
        pltpu.VMEM((model, 2, columns), BF16),
        pltpu.VMEM((model, 2 * columns), BF16),
        pltpu.VMEM((2 * block, model), BF16),
        pltpu.VMEM((2, 2 * block, model), BF16),
        pltpu.VMEM((2, rim, columns), BF16),
        pltpu.VMEM((2, rim, columns), BF16),
        dma((half,)),
        dma((half,)),
        dma((ny,)),
        dma((half,)),
        dma((nx, half)),
        dma((half,)),
        dma((half,)),
        dma((half,)),
        dma((half,)),
        dma((half,)),
        dma((half, 2)),
        dma((ny,)),
        dma,
        dma,
        dma((9,)),
        dma((2,)),
        dma((2,)),
        dma,
        dma,
        dma((pieces,)),
        dma((pieces,)),
        dma((pieces,)),
        dma((pieces,)),
        dma((2, pieces)),
        dma((2, pieces)),
        dma((2,)),
        dma((2,)),
    ]
    attended, padded = pl.pallas_call(
        functools.partial(kernel, ny, nx),
        out_shape=(
            jax.ShapeDtypeStruct((block, model), BF16),
            jax.ShapeDtypeStruct((rows + 2 * rim, columns), F32),
        ),
        in_specs=[anywhere] * 8,
        out_specs=(vmem, vmem),
        scratch_shapes=scratch,
        compiler_params=pltpu.CompilerParams(
            collective_id=0, has_side_effects=True, vmem_limit_bytes=56 * 1024 * 1024
        ),
        cost_estimate=pl.CostEstimate(
            flops=3 * 10**9, bytes_accessed=10**7, transcendentals=5 * 10**6
        ),
    )(
        residual_in,
        queries,
        keys,
        values,
        out_weight,
        norm_gain,
        norm_bias,
        glu_weight,
    )
    return pl.pallas_call(
        convolve,
        out_shape=(
            jax.ShapeDtypeStruct((block, model), BF16),
            jax.ShapeDtypeStruct((rows, columns), BF16),
        ),
        in_specs=[vmem] * 5,
        out_specs=(vmem, vmem),
    )(attended, padded, conv_weight, conv_scale, conv_shift)


def solution(mesh):
    return jax.shard_map(
        functools.partial(shards, mesh.shape["ctx"]),
        mesh=mesh,
        in_specs=(
            P(("dp", "ctx"), None),
            P(("dp", "ctx"), "tp"),
            P(("dp", "ctx"), "tp"),
            P(("dp", "ctx"), "tp"),
            P("tp", None),
            P(),
            P(),
            P(None, None, "tp"),
            P(None, "tp"),
            P("tp"),
            P("tp"),
        ),
        out_specs=(P(("dp", "ctx", "tp"), None), P(("dp", "ctx"), "tp")),
        check_vma=False,
    )
```

```python
import functools
import math

import jax
import jax.numpy as jnp
from jax import lax
from jax.experimental import pallas as pl
from jax.experimental.pallas import tpu as pltpu
from jax.sharding import PartitionSpec as P

KERNEL = 31
HD = 96
LANES = 128
MESH = pl.DeviceIdType.MESH
F32 = jnp.float32
BF16 = jnp.bfloat16


def wait_for(ref, sem):
    pltpu.make_async_copy(ref, ref, sem).wait()


def send(src, dst, send_sem, recv_sem, device):
    pltpu.make_async_remote_copy(
        src_ref=src,
        dst_ref=dst,
        send_sem=send_sem,
        recv_sem=recv_sem,
        device_id=device,
        device_id_type=MESH,
    ).start()


def send_or_keep(here, src, dst, send_sem, recv_sem, device):
    @pl.when(here)
    def _():
        pltpu.make_async_copy(src, dst, recv_sem).start()

    @pl.when(jnp.logical_not(here))
    def _():
        send(src, dst, send_sem, recv_sem, device)


def kernel(
    ny,
    nx,
    resid_in,
    q_in,
    k_in,
    v_in,
    w_ref,
    gain_in,
    bias_in,
    glu_ref,
    att_ref,
    gpad,
    q_ref,
    k_ref,
    v_ref,
    gain_ref,
    bias_ref,
    qs,
    kvs,
    qbuf,
    kvbuf,
    qfull,
    vfull,
    top,
    acc,
    accr,
    ctxs,
    cbuf,
    cat,
    wall,
    graw,
    gw,
    resid,
    nbuf,
    hs,
    hr,
    sq_s,
    skv_s,
    q_r,
    qf_s,
    kv_r,
    xr_s,
    xl_s,
    xf_s,
    a_s,
    a_r,
    c_s,
    c_r,
    w_s,
    w_r,
    l_r,
    z_s,
    z_r,
    n_s,
    n_r,
    wa_s,
    wa_r,
    wb_s,
    wb_r,
    wf_s,
    wf_r,
    h_s,
    h_r,
):
    half = ny // 2
    rows = q_in.shape[0]
    block = rows // 4
    rim = gpad.shape[0] - rows
    rim = rim // 2
    width = gpad.shape[1]
    dp = lax.axis_index("dp")
    ctx = lax.axis_index("ctx")
    tp = lax.axis_index("tp")
    n_ctx = ny * nx
    y, x = ctx // nx, ctx % nx
    zh, core = tp // 2, tp % 2
    parity = y % 2

    def dev(yy, xx, tt):
        return (dp, yy * nx + xx, tt)

    sibling = (dp, ctx, zh * 2 + 1 - core)
    away, away_sibling = (1 - zh) * 2 + core, (1 - zh) * 2 + 1 - core
    partner = (dp, ctx, away)
    n_dp = lax.axis_size("dp")
    above = (zh * n_dp + dp + 1) % (2 * n_dp)
    below = (zh * n_dp + dp + 2 * n_dp - 1) % (2 * n_dp)
    up = (above % n_dp, ctx, above // n_dp * 2 + core)
    down = (below % n_dp, ctx, below // n_dp * 2 + core)
    x_right, x_left, x_far = (x + 1) % nx, (x + nx - 1) % nx, (x + 2) % nx
    right, left = dev(y, x_right, tp), dev(y, x_left, tp)

    loads = [
        pltpu.make_async_copy(src, dst, l_r.at[i])
        for i, (src, dst) in enumerate(
            (
                (k_in, k_ref),
                (v_in, v_ref),
                (q_in, q_ref),
                (w_ref, wall.at[tp]),
                (glu_ref, graw),
                (resid_in.at[pl.ds(pl.multiple_of(core * block, block), block)], resid.at[0:block]),
                (
                    resid_in.at[pl.ds(pl.multiple_of((2 + core) * block, block), block)],
                    resid.at[block : 2 * block],
                ),
                (gain_in, gain_ref),
                (bias_in, bias_ref),
            )
        )
    ]
    load_k, load_v, load_q, own_w, own_g, own_x, own_x2, load_gain, load_bias = loads
    for load in loads:
        load.start()
    barrier = pltpu.get_barrier_semaphore()

    def greet(device):
        pl.semaphore_signal(barrier, inc=1, device_id=device, device_id_type=MESH)

    for o in range(1, ny):
        for cc in range(2):
            greet(dev((y + o) % ny, x, zh * 2 + cc))
    greet(sibling)
    greet(partner)
    greet(up)
    greet(down)
    greet(right)
    greet(left)
    greet((dp, (ctx + 1) % n_ctx, tp))
    greet((dp, (ctx + n_ctx - 1) % n_ctx, tp))

    cut = rows * 3 // 4
    part = rows - cut
    load_k.wait()
    load_v.wait()
    for j in range(half):
        lo = HD * j
        kvs[j, 0:rows] = jnp.concatenate(
            [k_ref[:, lo : lo + HD], v_ref[:, lo : lo + 32]], axis=1
        )
        kvs[j, rows : rows + rows // 2] = jnp.concatenate(
            [v_ref[0 : rows // 2, lo + 32 : lo + HD], v_ref[rows // 2 : rows, lo + 32 : lo + HD]],
            axis=1,
        )

    pl.semaphore_wait(barrier, 2 * (ny - 1) + 8)

    def rank(distance):
        sign = distance // (half + 1)
        fold = distance + sign * (ny - 2 * distance)
        odd = distance % 2
        return odd * (fold // 2 * 2 + sign) + (1 - odd) * (fold // 2 + fold // half + sign)

    near = [0]
    for o in range(1, half):
        near += [o, ny - o]
    near.append(half)

    def to_head(o, src, dst, send_sem, recv_sem):
        head = (y + o) % ny
        j = head % half
        device = dev(head, x, zh * 2 + parity)

        @pl.when(head // half == core)
        def _():
            if o == 0:
                send_or_keep(core == parity, src.at[j], dst, send_sem.at[j], recv_sem, device)
            else:
                send(src.at[j], dst, send_sem.at[j], recv_sem, device)

    def kv_to_head(o):
        place = rank((ny - o) % ny)
        to_head(o, kvs, kvbuf.at[x, place], skv_s, kv_r.at[x, place])

    for o in near[:3]:
        kv_to_head(o)
    pieces = wa_s.shape[0]
    piece_rows = w_ref.shape[0] // (2 * pieces)

    def piece_of(ref, side, i):
        start = side * (w_ref.shape[0] // 2) + i * piece_rows
        return ref.at[pl.ds(pl.multiple_of(start, 16), piece_rows)]

    def relay(slot):
        for side, hop, s_sem, r_sem, target in (
            (0, n_dp - 1 - dp, wa_s, wa_r, down),
            (1, dp, wb_s, wb_r, up),
        ):
            i = slot - hop

            @pl.when(jnp.logical_and(i >= 0, i < pieces))
            def _():
                held = piece_of(wall.at[away], side, i)
                wait_for(held, r_sem.at[i])

                @pl.when(hop < n_dp - 1)
                def _():
                    send(held, held, s_sem.at[i], r_sem.at[i], target)

                send(held, held, wf_s.at[side, i], wf_r.at[side, i], sibling)

    load_q.wait()
    for j in range(half):
        lo = HD * j
        qs[j] = jnp.concatenate(
            [
                q_ref[0:cut, lo : lo + HD],
                jnp.concatenate(
                    [q_ref[cut:rows, lo + 32 * i : lo + 32 * (i + 1)] for i in range(3)], axis=0
                ),
            ],
            axis=1,
        )
    for o in near[::-1]:
        to_head(o, qs, qbuf.at[y], sq_s, q_r.at[y])
    for o in near[3:]:
        kv_to_head(o)

    @pl.when(dp == 0)
    def _():
        for i in range(pieces):
            src, dst = piece_of(w_ref, 0, i), piece_of(wall.at[tp], 0, i)
            send(src, dst, wa_s.at[i], wa_r.at[i], down)

    @pl.when(dp == n_dp - 1)
    def _():
        for i in range(pieces):
            src, dst = piece_of(w_ref, 1, i), piece_of(wall.at[tp], 1, i)
            send(src, dst, wb_s.at[i], wb_r.at[i], up)

    def spread(s):
        wait_for(kvbuf.at[x, s], kv_r.at[x, s])
        send(kvbuf.at[x, s], kvbuf.at[x, s], xr_s.at[s], kv_r.at[x, s], right)
        send(kvbuf.at[x, s], kvbuf.at[x, s], xl_s.at[s], kv_r.at[x, s], left)

    def pass_on(s):
        slot, target = (x_left, right) if s % 2 == 0 else (x_right, left)
        wait_for(kvbuf.at[slot, s], kv_r.at[slot, s])
        send(kvbuf.at[slot, s], kvbuf.at[slot, s], xf_s.at[s], kv_r.at[slot, s], target)

    def arrive(slot, s):
        wait_for(kvbuf.at[slot, s], kv_r.at[slot, s])

    span = graw.shape[0] // half

    def relayout(i):
        @pl.loop(0, span // 16)
        def _(r):
            at = pl.ds(pl.multiple_of(i * span + r * 16, 16), 16)
            pair = graw[at].astype(F32)
            gw[at] = jnp.concatenate([pair[:, 0, :], pair[:, 1, :]], axis=1).astype(BF16)

    spread(0)
    for i in range(half):
        ys = 2 * ((y // 2 + i + 1) % half) + core
        wait_for(qbuf.at[ys], q_r.at[ys])
        send(qbuf.at[ys], qbuf.at[ys], qf_s.at[i], q_r.at[ys], sibling)
    own_g.wait()
    relayout(0)
    spread(1)
    send(w_ref, wall.at[tp], w_s, w_r, sibling)
    relayout(1)
    pass_on(0)
    for i in range(half):
        ys = 2 * ((y // 2 + i) % half) + 1 - core
        wait_for(qbuf.at[ys], q_r.at[ys])

    @pl.loop(0, ny)
    def _(t):
        base = pl.multiple_of(t * rows, rows)
        qfull[pl.ds(base, cut)] = jnp.concatenate(
            [qbuf[t, :, 0:HD], jnp.zeros((cut, LANES - HD), BF16)], axis=1
        )
        qfull[pl.ds(base + cut, part)] = jnp.concatenate(
            [qbuf[t, part * i : part * (i + 1), HD:LANES] for i in range(3)]
            + [jnp.zeros((part, LANES - HD), BF16)],
            axis=1,
        )

    pass_on(1)
    relayout(2)
    factor = math.log2(math.e) / math.sqrt(HD)
    hr_rows = rows // 2
    tall = rows + hr_rows

    quarter = half // 2

    def unpack(slots, first_place):
        ones = jnp.ones((hr_rows, LANES - HD), BF16)
        for n, slot in enumerate(slots):
            for m in range(quarter):
                for b in range(2):
                    base = (n * quarter + m) * rows + b * hr_rows
                    vfull[base : base + hr_rows] = jnp.concatenate(
                        [
                            kvbuf[slot, first_place + m, b * hr_rows : (b + 1) * hr_rows, HD:LANES],
                            kvbuf[slot, first_place + m, rows:tall, 64 * b : 64 * (b + 1)],
                            ones,
                        ],
                        axis=1,
                    )

    wide = 2 * rows

    def tile(slots, place, base, first):
        at = pl.ds(pl.multiple_of(base, wide), wide)
        kk = jnp.concatenate(
            [
                kvbuf[slot, place : place + quarter, 0:rows, :].reshape(quarter * rows, LANES)
                for slot in slots
            ],
            axis=0,
        )
        s = lax.dot_general(
            qfull[at], kk, (((1,), (1,)), ((), ())), preferred_element_type=F32
        )
        peak = jnp.max(s, axis=1, keepdims=True) * factor
        if first:
            new = peak
        else:
            old = top[at][:, 0:1]
            new = jnp.maximum(old, peak)
        p = jnp.exp2(s * factor - new)
        mix = jnp.dot(p.astype(BF16), vfull[...], preferred_element_type=F32)
        if not first:
            mix = mix + acc[at] * jnp.exp2(old - new)
        return at, mix, new

    def attend(slots, place, first):
        unpack(slots, place)
        for t in range(half):
            at, mix, new = tile(slots, place, t * wide, first)
            acc[at] = mix
            top[at] = jnp.broadcast_to(new, (wide, LANES))

    relay(0)
    arrive(x_left, 1)
    attend((x, x_left), 0, True)
    relay(1)
    spread(2)
    relayout(3)
    spread(3)
    arrive(x_right, 0)
    arrive(x_far, 0)
    arrive(x_far, 1)
    attend((x_right, x_far), 0, False)
    relay(2)
    pass_on(2)
    pass_on(3)
    arrive(x_left, 3)
    attend((x, x_left), 2, False)
    relay(3)
    arrive(x_right, 2)
    arrive(x_far, 2)
    arrive(x_far, 3)
    last = (x_right, x_far)
    unpack(last, 2)
    lane = lax.broadcasted_iota(jnp.int32, (wide, LANES), 1)
    for t in range(half // 2):
        at, mix, new = tile(last, 2, (1 - core) * half * rows + t * wide, False)
        acc[at] = jnp.where(lane >= LANES - 16, jnp.broadcast_to(new, (wide, LANES)), mix)
        send(acc.at[at], accr.at[pl.ds(t * wide, wide)], a_s.at[t], a_r.at[t], sibling)
    relay(4)
    for t in range(half // 2):
        at, mix, new = tile(last, 2, core * half * rows + t * wide, False)
        acc[at] = mix
        top[at] = jnp.broadcast_to(new, (wide, LANES))
    relay(5)
    for t in range(half // 2):
        wait_for(accr.at[pl.ds(t * wide, wide)], a_r.at[t])
        for k in range(2 * t, 2 * t + 2):
            yd = core * half + k
            at = pl.ds(pl.multiple_of(yd * rows, rows), rows)
            other = accr[k * rows : (k + 1) * rows]
            other_top = other[:, LANES - 1 : LANES]
            new = top[at][:, 0:1]
            both = jnp.maximum(new, other_top)
            total = acc[at] * jnp.exp2(new - both) + other * jnp.exp2(other_top - both)
            out = (total / total[:, HD : HD + 1]).astype(BF16)
            for cc in range(2):
                for zz in range(2):
                    src = (zz * 2 + cc) * block
                    ctxs[k, cc, zz * block : (zz + 1) * block] = out[src : src + block]
            for cc in range(2):
                send_or_keep(
                    jnp.logical_and(yd == y, core == cc),
                    ctxs.at[k, cc],
                    cbuf.at[y],
                    c_s.at[k, cc],
                    c_r.at[y],
                    dev(yd, x, zh * 2 + cc),
                )

    relay(6)
    for load in (own_w, own_x, own_x2, load_gain, load_bias):
        load.wait()
    wait_for(wall.at[zh * 2 + 1 - core], w_r)
    total = resid[...].astype(F32)
    for g in range(2):
        for j in range(half):
            wait_for(cbuf.at[g * half + j], c_r.at[g * half + j])
            cat[zh, g, :, HD * j : HD * (j + 1)] = cbuf[g * half + j, :, 0:HD]
        send(cat.at[zh, g], cat.at[zh, g], z_s.at[g], z_r.at[g], partner)
    relay(7)
    for g in range(2):
        total += jnp.dot(cat[zh, g], wall[zh * 2 + g], preferred_element_type=F32)
    for slot in range(8, n_dp + pieces - 1):
        relay(slot)
    for side in range(2):
        for i in range(pieces):
            wait_for(piece_of(wall.at[away_sibling], side, i), wf_r.at[side, i])
    for g in range(2):
        wait_for(cat.at[1 - zh, g], z_r.at[g])
        total += jnp.dot(cat[1 - zh, g], wall[(1 - zh) * 2 + g], preferred_element_type=F32)
    attended = total.astype(BF16)
    resid[...] = attended
    att_ref[...] = resid[pl.ds(pl.multiple_of(zh * block, block), block)]
    full = attended.astype(F32)
    centred = full - jnp.mean(full, axis=1, keepdims=True)
    var = jnp.mean(centred * centred, axis=1, keepdims=True)
    normed = centred * lax.rsqrt(var + 1e-05) * gain_ref[...].reshape(1, -1)
    nbuf[core] = (normed + bias_ref[...].reshape(1, -1)).astype(BF16)
    send(nbuf.at[core], nbuf.at[core], n_s, n_r, sibling)

    def gate(cc):
        projected = jnp.dot(nbuf[cc], gw[...], preferred_element_type=F32)
        gated = projected[:, 0:width] * jax.nn.sigmoid(projected[:, width:])
        gated = gated.astype(BF16).astype(F32)
        for zz in range(2):
            base = pl.multiple_of(rim + (zz * 2 + cc) * block, 16)
            gpad[pl.ds(base, block)] = gated[zz * block : (zz + 1) * block]
        edge = pl.multiple_of(rim + cc * (rows - rim), 16)
        hs[cc] = gpad[pl.ds(edge, rim)].astype(BF16)
        target = ctx + 2 * cc - 1

        @pl.when(jnp.logical_and(target >= 0, target < n_ctx))
        def _():
            send(hs.at[cc], hr.at[1 - cc], h_s.at[cc], h_r.at[1 - cc], (dp, target, tp))

    gate(core)
    wait_for(nbuf.at[1 - core], n_r)
    gate(1 - core)

    for side in range(2):
        source = ctx + 2 * side - 1
        exists = jnp.logical_and(source >= 0, source < n_ctx)
        place = pl.ds(side * (rim + rows), rim)

        @pl.when(exists)
        def _():
            wait_for(hr.at[side], h_r.at[side])
            gpad[place] = hr[side].astype(F32)

        @pl.when(jnp.logical_not(exists))
        def _():
            gpad[place] = jnp.zeros((rim, width), F32)

    for j in range(half):
        here = jnp.logical_and(core * half + j == y, core == parity)

        @pl.when(jnp.logical_not(here))
        def _():
            wait_for(qs.at[j], sq_s.at[j])
            wait_for(kvs.at[j], skv_s.at[j])

        wait_for(qbuf.at[j], qf_s.at[j])
        wait_for(kvbuf.at[x, j], xr_s.at[j])
        wait_for(kvbuf.at[x, j], xl_s.at[j])
        wait_for(kvbuf.at[x, j], xf_s.at[j])
        for cc in range(2):

            @pl.when(jnp.logical_not(jnp.logical_and(core * half + j == y, core == cc)))
            def _():
                wait_for(ctxs.at[j, cc], c_s.at[j, cc])

    wait_for(wall.at[tp], w_s)
    for t in range(half // 2):
        wait_for(accr.at[pl.ds(t * wide, wide)], a_s.at[t])
    for i in range(pieces):
        wait_for(piece_of(w_ref, 0, i), wa_s.at[i])
        wait_for(piece_of(w_ref, 1, i), wb_s.at[i])
        for side in range(2):
            wait_for(piece_of(w_ref, side, i), wf_s.at[side, i])
    for g in range(2):
        wait_for(cat.at[zh, g], z_s.at[g])
    wait_for(nbuf.at[core], n_s)
    for side in range(2):
        target = ctx + 2 * side - 1

        @pl.when(jnp.logical_and(target >= 0, target < n_ctx))
        def _():
            wait_for(hs.at[side], h_s.at[side])


def convolve(att_in, gpad, taps_ref, scale_ref, shift_ref, att_ref, conv_ref):
    rows = conv_ref.shape[0]
    rim = (gpad.shape[0] - rows) // 2
    att_ref[...] = att_in[...]
    offset = rim - (KERNEL - 1) // 2
    taps = taps_ref[...]
    scale = scale_ref[...].reshape(1, -1)
    shift = shift_ref[...].reshape(1, -1)

    for r in range(0, rows, 4 * rim):
        for lane in range(0, conv_ref.shape[1], LANES):
            at = slice(lane, lane + LANES)
            window = gpad[r : r + 6 * rim, at]
            total = None
            for turn in range(8):
                places = [p for p in range(offset, offset + KERNEL) if p % 8 == turn]
                top = places[-1] + 4 * rim
                turned = window[turn : turn + (top - turn) // 8 * 8]
                for p in places:
                    term = turned[p - turn : p - turn + 4 * rim] * taps[p - offset : p - offset + 1, at]
                    total = term if total is None else total + term
            u = total * scale[:, at] + shift[:, at]
            conv_ref[r : r + 4 * rim, at] = (u * jax.nn.sigmoid(u)).astype(BF16)


def shards(
    n_ctx,
    residual_in,
    queries,
    keys,
    values,
    out_weight,
    norm_gain,
    norm_bias,
    glu_weight,
    conv_weight,
    conv_scale,
    conv_shift,
):
    rows, columns = queries.shape
    half = columns // HD
    ny = 2 * half
    nx = n_ctx // ny
    model = residual_in.shape[1]
    block = rows // 4
    pieces = columns // 64
    rim = 16
    vmem = pl.BlockSpec(memory_space=pltpu.VMEM)
    anywhere = pl.BlockSpec(memory_space=pl.ANY)
    dma = pltpu.SemaphoreType.DMA
    tall = rows + rows // 2
    scratch = [
        pltpu.VMEM((rows, columns), BF16),
        pltpu.VMEM((rows, columns), BF16),
        pltpu.VMEM((rows, columns), BF16),
        pltpu.VMEM((model,), F32),
        pltpu.VMEM((model,), F32),
        pltpu.VMEM((half, rows * 3 // 4, LANES), BF16),
        pltpu.VMEM((half, tall, LANES), BF16),
        pltpu.VMEM((ny, rows * 3 // 4, LANES), BF16),
        pltpu.VMEM((nx, half, tall, LANES), BF16),
        pltpu.VMEM((ny * rows, LANES), BF16),
        pltpu.VMEM((half * rows, LANES), BF16),
        pltpu.VMEM((ny * rows, LANES), F32),
        pltpu.VMEM((ny * rows, LANES), F32),
        pltpu.VMEM((half * rows, LANES), F32),
        pltpu.VMEM((half, 2, 2 * block, LANES), BF16),
        pltpu.VMEM((ny, 2 * block, LANES), BF16),
        pltpu.VMEM((2, 2, 2 * block, columns), BF16),
        pltpu.VMEM((4, columns, model), BF16),
        pltpu.VMEM((model, 2, columns), BF16),
        pltpu.VMEM((model, 2 * columns), BF16),
        pltpu.VMEM((2 * block, model), BF16),
        pltpu.VMEM((2, 2 * block, model), BF16),
        pltpu.VMEM((2, rim, columns), BF16),
        pltpu.VMEM((2, rim, columns), BF16),
        dma((half,)),
        dma((half,)),
        dma((ny,)),
        dma((half,)),
        dma((nx, half)),
        dma((half,)),
        dma((half,)),
        dma((half,)),
        dma((half,)),
        dma((half,)),
        dma((half, 2)),
        dma((ny,)),
        dma,
        dma,
        dma((9,)),
        dma((2,)),
        dma((2,)),
        dma,
        dma,
        dma((pieces,)),
        dma((pieces,)),
        dma((pieces,)),
        dma((pieces,)),
        dma((2, pieces)),
        dma((2, pieces)),
        dma((2,)),
        dma((2,)),
    ]
    attended, padded = pl.pallas_call(
        functools.partial(kernel, ny, nx),
        out_shape=(
            jax.ShapeDtypeStruct((block, model), BF16),
            jax.ShapeDtypeStruct((rows + 2 * rim, columns), F32),
        ),
        in_specs=[anywhere] * 8,
        out_specs=(vmem, vmem),
        scratch_shapes=scratch,
        compiler_params=pltpu.CompilerParams(
            collective_id=0, has_side_effects=True, vmem_limit_bytes=56 * 1024 * 1024
        ),
        cost_estimate=pl.CostEstimate(
            flops=3 * 10**9, bytes_accessed=10**7, transcendentals=5 * 10**6
        ),
    )(
        residual_in,
        queries,
        keys,
        values,
        out_weight,
        norm_gain,
        norm_bias,
        glu_weight,
    )
    return pl.pallas_call(
        convolve,
        out_shape=(
            jax.ShapeDtypeStruct((block, model), BF16),
            jax.ShapeDtypeStruct((rows, columns), BF16),
        ),
        in_specs=[vmem] * 5,
        out_specs=(vmem, vmem),
    )(attended, padded, conv_weight, conv_scale, conv_shift)


def solution(mesh):
    return jax.shard_map(
        functools.partial(shards, mesh.shape["ctx"]),
        mesh=mesh,
        in_specs=(
            P(("dp", "ctx"), None),
            P(("dp", "ctx"), "tp"),
            P(("dp", "ctx"), "tp"),
            P(("dp", "ctx"), "tp"),
            P("tp", None),
            P(),
            P(),
            P(None, None, "tp"),
            P(None, "tp"),
            P("tp"),
            P("tp"),
        ),
        out_specs=(P(("dp", "ctx", "tp"), None), P(("dp", "ctx"), "tp")),
        check_vma=False,
    )
```

```python
import functools
import math

import jax
import jax.numpy as jnp
from jax import lax
from jax.experimental import pallas as pl
from jax.experimental.pallas import tpu as pltpu
from jax.sharding import PartitionSpec as P

KERNEL = 31
HD = 96
LANES = 128
MESH = pl.DeviceIdType.MESH
F32 = jnp.float32
BF16 = jnp.bfloat16


def wait_for(ref, sem):
    pltpu.make_async_copy(ref, ref, sem).wait()


def send(src, dst, send_sem, recv_sem, device):
    pltpu.make_async_remote_copy(
        src_ref=src,
        dst_ref=dst,
        send_sem=send_sem,
        recv_sem=recv_sem,
        device_id=device,
        device_id_type=MESH,
    ).start()


def send_or_keep(here, src, dst, send_sem, recv_sem, device):
    @pl.when(here)
    def _():
        pltpu.make_async_copy(src, dst, recv_sem).start()

    @pl.when(jnp.logical_not(here))
    def _():
        send(src, dst, send_sem, recv_sem, device)


def kernel(
    ny,
    nx,
    resid_in,
    q_in,
    k_in,
    v_in,
    w_ref,
    gain_in,
    bias_in,
    glu_ref,
    att_ref,
    gpad,
    q_ref,
    k_ref,
    v_ref,
    gain_ref,
    bias_ref,
    qs,
    kvs,
    qbuf,
    kvbuf,
    qfull,
    vfull,
    top,
    acc,
    accr,
    ctxs,
    cbuf,
    cat,
    wall,
    graw,
    gw,
    resid,
    nbuf,
    hs,
    hr,
    sq_s,
    skv_s,
    q_r,
    qf_s,
    kv_r,
    xr_s,
    xl_s,
    xf_s,
    a_s,
    a_r,
    c_s,
    c_r,
    w_s,
    ww_r,
    l_r,
    z_s,
    z_r,
    n_s,
    n_r,
    wa_s,
    w_r,
    wb_s,
    wf_s,
    wf_r,
    h_s,
    h_r,
):
    half = ny // 2
    rows = q_in.shape[0]
    block = rows // 4
    rim = gpad.shape[0] - rows
    rim = rim // 2
    width = gpad.shape[1]
    dp = lax.axis_index("dp")
    ctx = lax.axis_index("ctx")
    tp = lax.axis_index("tp")
    n_ctx = ny * nx
    y, x = ctx // nx, ctx % nx
    zh, core = tp // 2, tp % 2
    parity = y % 2

    def dev(yy, xx, tt):
        return (dp, yy * nx + xx, tt)

    sibling = (dp, ctx, zh * 2 + 1 - core)
    away, away_sibling = (1 - zh) * 2 + core, (1 - zh) * 2 + 1 - core
    partner = (dp, ctx, away)
    n_dp = lax.axis_size("dp")
    above = (zh * n_dp + dp + 1) % (2 * n_dp)
    below = (zh * n_dp + dp + 2 * n_dp - 1) % (2 * n_dp)
    up = (above % n_dp, ctx, above // n_dp * 2 + core)
    down = (below % n_dp, ctx, below // n_dp * 2 + core)
    x_right, x_left, x_far = (x + 1) % nx, (x + nx - 1) % nx, (x + 2) % nx
    right, left = dev(y, x_right, tp), dev(y, x_left, tp)

    loads = [
        pltpu.make_async_copy(src, dst, l_r.at[i])
        for i, (src, dst) in enumerate(
            (
                (k_in, k_ref),
                (v_in, v_ref),
                (q_in, q_ref),
                (w_ref, wall.at[tp]),
                (glu_ref, graw),
                (resid_in.at[pl.ds(pl.multiple_of(core * block, block), block)], resid.at[0:block]),
                (
                    resid_in.at[pl.ds(pl.multiple_of((2 + core) * block, block), block)],
                    resid.at[block : 2 * block],
                ),
                (gain_in, gain_ref),
                (bias_in, bias_ref),
            )
        )
    ]
    load_k, load_v, load_q, own_w, own_g, own_x, own_x2, load_gain, load_bias = loads
    for load in loads:
        load.start()
    barrier = pltpu.get_barrier_semaphore()

    def greet(device):
        pl.semaphore_signal(barrier, inc=1, device_id=device, device_id_type=MESH)

    for o in range(1, ny):
        for cc in range(2):
            greet(dev((y + o) % ny, x, zh * 2 + cc))
    greet(sibling)
    greet(partner)
    greet(up)
    greet(down)
    greet(right)
    greet(left)
    greet((dp, (ctx + 1) % n_ctx, tp))
    greet((dp, (ctx + n_ctx - 1) % n_ctx, tp))

    cut = rows * 3 // 4
    part = rows - cut
    load_k.wait()
    load_v.wait()
    for j in range(half):
        lo = HD * j
        kvs[j, 0:rows] = jnp.concatenate(
            [k_ref[:, lo : lo + HD], v_ref[:, lo : lo + 32]], axis=1
        )
        kvs[j, rows : rows + rows // 2] = jnp.concatenate(
            [v_ref[0 : rows // 2, lo + 32 : lo + HD], v_ref[rows // 2 : rows, lo + 32 : lo + HD]],
            axis=1,
        )

    pl.semaphore_wait(barrier, 2 * (ny - 1) + 8)

    def rank(distance):
        sign = distance // (half + 1)
        fold = distance + sign * (ny - 2 * distance)
        odd = distance % 2
        return odd * (fold // 2 * 2 + sign) + (1 - odd) * (fold // 2 + fold // half + sign)

    near = [0]
    for o in range(1, half):
        near += [o, ny - o]
    near.append(half)

    def to_head(o, src, dst, send_sem, recv_sem):
        head = (y + o) % ny
        j = head % half
        device = dev(head, x, zh * 2 + parity)

        @pl.when(head // half == core)
        def _():
            if o == 0:
                send_or_keep(core == parity, src.at[j], dst, send_sem.at[j], recv_sem, device)
            else:
                send(src.at[j], dst, send_sem.at[j], recv_sem, device)

    def kv_to_head(o):
        place = rank((ny - o) % ny)
        to_head(o, kvs, kvbuf.at[x, place], skv_s, kv_r.at[x, place])

    for o in near[:3]:
        kv_to_head(o)
    pieces = wa_s.shape[0]
    piece_rows = w_ref.shape[0] // pieces

    def piece_of(ref, i):
        return ref.at[i * piece_rows : (i + 1) * piece_rows]

    low, high = dp == 0, dp == n_dp - 1
    edge = jnp.logical_or(low, high)

    def relay(i):
        held = piece_of(wall.at[away], i)

        @pl.when(edge)
        def _():
            wait_for(held, w_r.at[i])

        for on, device in ((low, up), (high, down)):

            @pl.when(on)
            def _():
                send(held, held, wb_s.at[i], w_r.at[i], device)

    def share(i):
        held = piece_of(wall.at[away], i)

        @pl.when(jnp.logical_not(edge))
        def _():
            wait_for(held, w_r.at[i])

        send(held, held, wf_s.at[i], wf_r.at[i], sibling)

    load_q.wait()
    for j in range(half):
        lo = HD * j
        qs[j] = jnp.concatenate(
            [
                q_ref[0:cut, lo : lo + HD],
                jnp.concatenate(
                    [q_ref[cut:rows, lo + 32 * i : lo + 32 * (i + 1)] for i in range(3)], axis=0
                ),
            ],
            axis=1,
        )
    for o in near[::-1]:
        to_head(o, qs, qbuf.at[y], sq_s, q_r.at[y])
    for o in near[3:]:
        kv_to_head(o)

    for on, device in ((low, down), (high, up)):

        @pl.when(on)
        def _():
            for i in range(pieces):
                src, dst = piece_of(w_ref, i), piece_of(wall.at[tp], i)
                send(src, dst, wa_s.at[i], w_r.at[i], device)

    def spread(s):
        wait_for(kvbuf.at[x, s], kv_r.at[x, s])
        send(kvbuf.at[x, s], kvbuf.at[x, s], xr_s.at[s], kv_r.at[x, s], right)
        send(kvbuf.at[x, s], kvbuf.at[x, s], xl_s.at[s], kv_r.at[x, s], left)

    def pass_on(s):
        slot, target = (x_left, right) if s % 2 == 0 else (x_right, left)
        wait_for(kvbuf.at[slot, s], kv_r.at[slot, s])
        send(kvbuf.at[slot, s], kvbuf.at[slot, s], xf_s.at[s], kv_r.at[slot, s], target)

    def arrive(slot, s):
        wait_for(kvbuf.at[slot, s], kv_r.at[slot, s])

    span = graw.shape[0] // half

    def relayout(i):
        @pl.loop(0, span // 16)
        def _(r):
            at = pl.ds(pl.multiple_of(i * span + r * 16, 16), 16)
            pair = graw[at].astype(F32)
            gw[at] = jnp.concatenate([pair[:, 0, :], pair[:, 1, :]], axis=1).astype(BF16)

    spread(0)
    for i in range(half):
        ys = 2 * ((y // 2 + i + 1) % half) + core
        wait_for(qbuf.at[ys], q_r.at[ys])
        send(qbuf.at[ys], qbuf.at[ys], qf_s.at[i], q_r.at[ys], sibling)
    own_g.wait()
    relayout(0)
    spread(1)
    send(w_ref, wall.at[tp], w_s, ww_r, sibling)
    relayout(1)
    pass_on(0)
    for i in range(half):
        ys = 2 * ((y // 2 + i) % half) + 1 - core
        wait_for(qbuf.at[ys], q_r.at[ys])

    @pl.loop(0, ny)
    def _(t):
        base = pl.multiple_of(t * rows, rows)
        qfull[pl.ds(base, cut)] = jnp.concatenate(
            [qbuf[t, :, 0:HD], jnp.zeros((cut, LANES - HD), BF16)], axis=1
        )
        qfull[pl.ds(base + cut, part)] = jnp.concatenate(
            [qbuf[t, part * i : part * (i + 1), HD:LANES] for i in range(3)]
            + [jnp.zeros((part, LANES - HD), BF16)],
            axis=1,
        )

    pass_on(1)
    relayout(2)
    factor = math.log2(math.e) / math.sqrt(HD)
    hr_rows = rows // 2
    tall = rows + hr_rows

    quarter = half // 2

    def unpack(slots, first_place):
        ones = jnp.ones((hr_rows, LANES - HD), BF16)
        for n, slot in enumerate(slots):
            for m in range(quarter):
                for b in range(2):
                    base = (n * quarter + m) * rows + b * hr_rows
                    vfull[base : base + hr_rows] = jnp.concatenate(
                        [
                            kvbuf[slot, first_place + m, b * hr_rows : (b + 1) * hr_rows, HD:LANES],
                            kvbuf[slot, first_place + m, rows:tall, 64 * b : 64 * (b + 1)],
                            ones,
                        ],
                        axis=1,
                    )

    wide = 2 * rows

    def tile(slots, place, base, first):
        at = pl.ds(pl.multiple_of(base, wide), wide)
        kk = jnp.concatenate(
            [
                kvbuf[slot, place : place + quarter, 0:rows, :].reshape(quarter * rows, LANES)
                for slot in slots
            ],
            axis=0,
        )
        s = lax.dot_general(
            qfull[at], kk, (((1,), (1,)), ((), ())), preferred_element_type=F32
        )
        peak = jnp.max(s, axis=1, keepdims=True) * factor
        if first:
            new = peak
        else:
            old = top[at][:, 0:1]
            new = jnp.maximum(old, peak)
        p = jnp.exp2(s * factor - new)
        mix = jnp.dot(p.astype(BF16), vfull[...], preferred_element_type=F32)
        if not first:
            mix = mix + acc[at] * jnp.exp2(old - new)
        return at, mix, new

    def attend(slots, place, first):
        unpack(slots, place)
        for t in range(half):
            at, mix, new = tile(slots, place, t * wide, first)
            acc[at] = mix
            top[at] = jnp.broadcast_to(new, (wide, LANES))

    relay(0)
    arrive(x_left, 1)
    attend((x, x_left), 0, True)
    relay(1)
    spread(2)
    relayout(3)
    spread(3)
    arrive(x_right, 0)
    arrive(x_far, 0)
    arrive(x_far, 1)
    attend((x_right, x_far), 0, False)
    relay(2)
    pass_on(2)
    pass_on(3)
    arrive(x_left, 3)
    attend((x, x_left), 2, False)
    relay(3)
    arrive(x_right, 2)
    arrive(x_far, 2)
    arrive(x_far, 3)
    last = (x_right, x_far)
    unpack(last, 2)
    lane = lax.broadcasted_iota(jnp.int32, (wide, LANES), 1)
    for t in range(half // 2):
        at, mix, new = tile(last, 2, (1 - core) * half * rows + t * wide, False)
        acc[at] = jnp.where(lane >= LANES - 16, jnp.broadcast_to(new, (wide, LANES)), mix)
        send(acc.at[at], accr.at[pl.ds(t * wide, wide)], a_s.at[t], a_r.at[t], sibling)
    for t in range(half // 2):
        at, mix, new = tile(last, 2, core * half * rows + t * wide, False)
        acc[at] = mix
        top[at] = jnp.broadcast_to(new, (wide, LANES))
    relay(4)
    for i in range(2):
        share(i)
    for t in range(half // 2):
        wait_for(accr.at[pl.ds(t * wide, wide)], a_r.at[t])
        for k in range(2 * t, 2 * t + 2):
            yd = core * half + k
            at = pl.ds(pl.multiple_of(yd * rows, rows), rows)
            other = accr[k * rows : (k + 1) * rows]
            other_top = other[:, LANES - 1 : LANES]
            new = top[at][:, 0:1]
            both = jnp.maximum(new, other_top)
            total = acc[at] * jnp.exp2(new - both) + other * jnp.exp2(other_top - both)
            out = (total / total[:, HD : HD + 1]).astype(BF16)
            for cc in range(2):
                for zz in range(2):
                    src = (zz * 2 + cc) * block
                    ctxs[k, cc, zz * block : (zz + 1) * block] = out[src : src + block]
            for cc in range(2):
                send_or_keep(
                    jnp.logical_and(yd == y, core == cc),
                    ctxs.at[k, cc],
                    cbuf.at[y],
                    c_s.at[k, cc],
                    c_r.at[y],
                    dev(yd, x, zh * 2 + cc),
                )

    relay(5)
    share(2)
    share(3)
    for load in (own_w, own_x, own_x2, load_gain, load_bias):
        load.wait()
    wait_for(wall.at[zh * 2 + 1 - core], ww_r)
    total = resid[...].astype(F32)
    for g in range(2):
        for j in range(half):
            wait_for(cbuf.at[g * half + j], c_r.at[g * half + j])
            cat[zh, g, :, HD * j : HD * (j + 1)] = cbuf[g * half + j, :, 0:HD]
        send(cat.at[zh, g], cat.at[zh, g], z_s.at[g], z_r.at[g], partner)
    for g in range(2):
        total += jnp.dot(cat[zh, g], wall[zh * 2 + g], preferred_element_type=F32)
    for i in range(4, pieces):
        share(i)
    for i in range(pieces):
        wait_for(piece_of(wall.at[away_sibling], i), wf_r.at[i])
    for g in range(2):
        wait_for(cat.at[1 - zh, g], z_r.at[g])
        total += jnp.dot(cat[1 - zh, g], wall[(1 - zh) * 2 + g], preferred_element_type=F32)
    attended = total.astype(BF16)
    resid[...] = attended
    att_ref[...] = resid[pl.ds(pl.multiple_of(zh * block, block), block)]
    full = attended.astype(F32)
    centred = full - jnp.mean(full, axis=1, keepdims=True)
    var = jnp.mean(centred * centred, axis=1, keepdims=True)
    normed = centred * lax.rsqrt(var + 1e-05) * gain_ref[...].reshape(1, -1)
    nbuf[core] = (normed + bias_ref[...].reshape(1, -1)).astype(BF16)
    send(nbuf.at[core], nbuf.at[core], n_s, n_r, sibling)

    def gate(cc):
        projected = jnp.dot(nbuf[cc], gw[...], preferred_element_type=F32)
        gated = projected[:, 0:width] * jax.nn.sigmoid(projected[:, width:])
        gated = gated.astype(BF16).astype(F32)
        for zz in range(2):
            base = pl.multiple_of(rim + (zz * 2 + cc) * block, 16)
            gpad[pl.ds(base, block)] = gated[zz * block : (zz + 1) * block]
        edge = pl.multiple_of(rim + cc * (rows - rim), 16)
        hs[cc] = gpad[pl.ds(edge, rim)].astype(BF16)
        target = ctx + 2 * cc - 1

        @pl.when(jnp.logical_and(target >= 0, target < n_ctx))
        def _():
            send(hs.at[cc], hr.at[1 - cc], h_s.at[cc], h_r.at[1 - cc], (dp, target, tp))

    gate(core)
    wait_for(nbuf.at[1 - core], n_r)
    gate(1 - core)

    for side in range(2):
        source = ctx + 2 * side - 1
        exists = jnp.logical_and(source >= 0, source < n_ctx)
        place = pl.ds(side * (rim + rows), rim)

        @pl.when(exists)
        def _():
            wait_for(hr.at[side], h_r.at[side])
            gpad[place] = hr[side].astype(F32)

        @pl.when(jnp.logical_not(exists))
        def _():
            gpad[place] = jnp.zeros((rim, width), F32)

    for j in range(half):
        here = jnp.logical_and(core * half + j == y, core == parity)

        @pl.when(jnp.logical_not(here))
        def _():
            wait_for(qs.at[j], sq_s.at[j])
            wait_for(kvs.at[j], skv_s.at[j])

        wait_for(qbuf.at[j], qf_s.at[j])
        wait_for(kvbuf.at[x, j], xr_s.at[j])
        wait_for(kvbuf.at[x, j], xl_s.at[j])
        wait_for(kvbuf.at[x, j], xf_s.at[j])
        for cc in range(2):

            @pl.when(jnp.logical_not(jnp.logical_and(core * half + j == y, core == cc)))
            def _():
                wait_for(ctxs.at[j, cc], c_s.at[j, cc])

    wait_for(wall.at[tp], w_s)
    for t in range(half // 2):
        wait_for(accr.at[pl.ds(t * wide, wide)], a_s.at[t])
    for i in range(pieces):
        wait_for(piece_of(w_ref, i), wf_s.at[i])

        @pl.when(edge)
        def _():
            wait_for(piece_of(w_ref, i), wa_s.at[i])
            wait_for(piece_of(w_ref, i), wb_s.at[i])

    for g in range(2):
        wait_for(cat.at[zh, g], z_s.at[g])
    wait_for(nbuf.at[core], n_s)
    for side in range(2):
        target = ctx + 2 * side - 1

        @pl.when(jnp.logical_and(target >= 0, target < n_ctx))
        def _():
            wait_for(hs.at[side], h_s.at[side])


def convolve(att_in, gpad, taps_ref, scale_ref, shift_ref, att_ref, conv_ref):
    rows = conv_ref.shape[0]
    rim = (gpad.shape[0] - rows) // 2
    att_ref[...] = att_in[...]
    offset = rim - (KERNEL - 1) // 2
    taps = taps_ref[...]
    scale = scale_ref[...].reshape(1, -1)
    shift = shift_ref[...].reshape(1, -1)

    for r in range(0, rows, 4 * rim):
        for lane in range(0, conv_ref.shape[1], LANES):
            at = slice(lane, lane + LANES)
            window = gpad[r : r + 6 * rim, at]
            total = None
            for turn in range(8):
                places = [p for p in range(offset, offset + KERNEL) if p % 8 == turn]
                top = places[-1] + 4 * rim
                turned = window[turn : turn + (top - turn) // 8 * 8]
                for p in places:
                    term = turned[p - turn : p - turn + 4 * rim] * taps[p - offset : p - offset + 1, at]
                    total = term if total is None else total + term
            u = total * scale[:, at] + shift[:, at]
            conv_ref[r : r + 4 * rim, at] = (u * jax.nn.sigmoid(u)).astype(BF16)


def shards(
    n_ctx,
    residual_in,
    queries,
    keys,
    values,
    out_weight,
    norm_gain,
    norm_bias,
    glu_weight,
    conv_weight,
    conv_scale,
    conv_shift,
):
    rows, columns = queries.shape
    half = columns // HD
    ny = 2 * half
    nx = n_ctx // ny
    model = residual_in.shape[1]
    block = rows // 4
    pieces = columns // 64
    rim = 16
    vmem = pl.BlockSpec(memory_space=pltpu.VMEM)
    anywhere = pl.BlockSpec(memory_space=pl.ANY)
    dma = pltpu.SemaphoreType.DMA
    tall = rows + rows // 2
    scratch = [
        pltpu.VMEM((rows, columns), BF16),
        pltpu.VMEM((rows, columns), BF16),
        pltpu.VMEM((rows, columns), BF16),
        pltpu.VMEM((model,), F32),
        pltpu.VMEM((model,), F32),
        pltpu.VMEM((half, rows * 3 // 4, LANES), BF16),
        pltpu.VMEM((half, tall, LANES), BF16),
        pltpu.VMEM((ny, rows * 3 // 4, LANES), BF16),
        pltpu.VMEM((nx, half, tall, LANES), BF16),
        pltpu.VMEM((ny * rows, LANES), BF16),
        pltpu.VMEM((half * rows, LANES), BF16),
        pltpu.VMEM((ny * rows, LANES), F32),
        pltpu.VMEM((ny * rows, LANES), F32),
        pltpu.VMEM((half * rows, LANES), F32),
        pltpu.VMEM((half, 2, 2 * block, LANES), BF16),
        pltpu.VMEM((ny, 2 * block, LANES), BF16),
        pltpu.VMEM((2, 2, 2 * block, columns), BF16),
        pltpu.VMEM((4, columns, model), BF16),
        pltpu.VMEM((model, 2, columns), BF16),
        pltpu.VMEM((model, 2 * columns), BF16),
        pltpu.VMEM((2 * block, model), BF16),
        pltpu.VMEM((2, 2 * block, model), BF16),
        pltpu.VMEM((2, rim, columns), BF16),
        pltpu.VMEM((2, rim, columns), BF16),
        dma((half,)),
        dma((half,)),
        dma((ny,)),
        dma((half,)),
        dma((nx, half)),
        dma((half,)),
        dma((half,)),
        dma((half,)),
        dma((half,)),
        dma((half,)),
        dma((half, 2)),
        dma((ny,)),
        dma,
        dma,
        dma((9,)),
        dma((2,)),
        dma((2,)),
        dma,
        dma,
        dma((pieces,)),
        dma((pieces,)),
        dma((pieces,)),
        dma((pieces,)),
        dma((pieces,)),
        dma((2,)),
        dma((2,)),
    ]
    attended, padded = pl.pallas_call(
        functools.partial(kernel, ny, nx),
        out_shape=(
            jax.ShapeDtypeStruct((block, model), BF16),
            jax.ShapeDtypeStruct((rows + 2 * rim, columns), F32),
        ),
        in_specs=[anywhere] * 8,
        out_specs=(vmem, vmem),
        scratch_shapes=scratch,
        compiler_params=pltpu.CompilerParams(
            collective_id=0, has_side_effects=True, vmem_limit_bytes=56 * 1024 * 1024
        ),
        cost_estimate=pl.CostEstimate(
            flops=3 * 10**9, bytes_accessed=10**7, transcendentals=5 * 10**6
        ),
    )(
        residual_in,
        queries,
        keys,
        values,
        out_weight,
        norm_gain,
        norm_bias,
        glu_weight,
    )
    return pl.pallas_call(
        convolve,
        out_shape=(
            jax.ShapeDtypeStruct((block, model), BF16),
            jax.ShapeDtypeStruct((rows, columns), BF16),
        ),
        in_specs=[vmem] * 5,
        out_specs=(vmem, vmem),
    )(attended, padded, conv_weight, conv_scale, conv_shift)


def solution(mesh):
    return jax.shard_map(
        functools.partial(shards, mesh.shape["ctx"]),
        mesh=mesh,
        in_specs=(
            P(("dp", "ctx"), None),
            P(("dp", "ctx"), "tp"),
            P(("dp", "ctx"), "tp"),
            P(("dp", "ctx"), "tp"),
            P("tp", None),
            P(),
            P(),
            P(None, None, "tp"),
            P(None, "tp"),
            P("tp"),
            P("tp"),
        ),
        out_specs=(P(("dp", "ctx", "tp"), None), P(("dp", "ctx"), "tp")),
        check_vma=False,
    )
```

```python
import functools
import math

import jax
import jax.numpy as jnp
from jax import lax
from jax.experimental import pallas as pl
from jax.experimental.pallas import tpu as pltpu
from jax.sharding import PartitionSpec as P

KERNEL = 31
HD = 96
LANES = 128
MESH = pl.DeviceIdType.MESH
F32 = jnp.float32
BF16 = jnp.bfloat16


def wait_for(ref, sem):
    pltpu.make_async_copy(ref, ref, sem).wait()


def send(src, dst, send_sem, recv_sem, device):
    pltpu.make_async_remote_copy(
        src_ref=src,
        dst_ref=dst,
        send_sem=send_sem,
        recv_sem=recv_sem,
        device_id=device,
        device_id_type=MESH,
    ).start()


def send_or_keep(here, src, dst, send_sem, recv_sem, device):
    @pl.when(here)
    def _():
        pltpu.make_async_copy(src, dst, recv_sem).start()

    @pl.when(jnp.logical_not(here))
    def _():
        send(src, dst, send_sem, recv_sem, device)


def kernel(
    ny,
    nx,
    resid_in,
    q_in,
    k_in,
    v_in,
    w_ref,
    gain_in,
    bias_in,
    glu_ref,
    att_ref,
    gpad,
    q_ref,
    k_ref,
    v_ref,
    gain_ref,
    bias_ref,
    qs,
    kvs,
    qbuf,
    kvbuf,
    qfull,
    vfull,
    top,
    acc,
    accr,
    ctxs,
    cbuf,
    cat,
    wall,
    graw,
    gw,
    resid,
    nbuf,
    hs,
    hr,
    sq_s,
    skv_s,
    q_r,
    qf_s,
    kv_r,
    xr_s,
    xl_s,
    xf_s,
    a_s,
    a_r,
    c_s,
    c_r,
    w_s,
    ww_r,
    l_r,
    z_s,
    z_r,
    n_s,
    n_r,
    wa_s,
    w_r,
    wb_s,
    wf_s,
    wf_r,
    h_s,
    h_r,
):
    half = ny // 2
    rows = q_in.shape[0]
    block = rows // 4
    rim = gpad.shape[0] - rows
    rim = rim // 2
    width = gpad.shape[1]
    dp = lax.axis_index("dp")
    ctx = lax.axis_index("ctx")
    tp = lax.axis_index("tp")
    n_ctx = ny * nx
    y, x = ctx // nx, ctx % nx
    zh, core = tp // 2, tp % 2
    parity = y % 2

    def dev(yy, xx, tt):
        return (dp, yy * nx + xx, tt)

    sibling = (dp, ctx, zh * 2 + 1 - core)
    away, away_sibling = (1 - zh) * 2 + core, (1 - zh) * 2 + 1 - core
    partner = (dp, ctx, away)
    n_dp = lax.axis_size("dp")
    above = (zh * n_dp + dp + 1) % (2 * n_dp)
    below = (zh * n_dp + dp + 2 * n_dp - 1) % (2 * n_dp)
    up = (above % n_dp, ctx, above // n_dp * 2 + core)
    down = (below % n_dp, ctx, below // n_dp * 2 + core)
    x_right, x_left, x_far = (x + 1) % nx, (x + nx - 1) % nx, (x + 2) % nx
    right, left, far = dev(y, x_right, tp), dev(y, x_left, tp), dev(y, x_far, tp)

    loads = [
        pltpu.make_async_copy(src, dst, l_r.at[i])
        for i, (src, dst) in enumerate(
            (
                (k_in, k_ref),
                (v_in, v_ref),
                (q_in, q_ref),
                (w_ref, wall.at[tp]),
                (glu_ref, graw),
                (resid_in.at[pl.ds(pl.multiple_of(core * block, block), block)], resid.at[0:block]),
                (
                    resid_in.at[pl.ds(pl.multiple_of((2 + core) * block, block), block)],
                    resid.at[block : 2 * block],
                ),
                (gain_in, gain_ref),
                (bias_in, bias_ref),
            )
        )
    ]
    load_k, load_v, load_q, own_w, own_g, own_x, own_x2, load_gain, load_bias = loads
    for load in loads:
        load.start()
    barrier = pltpu.get_barrier_semaphore()

    def greet(device):
        pl.semaphore_signal(barrier, inc=1, device_id=device, device_id_type=MESH)

    for o in range(1, ny):
        for cc in range(2):
            greet(dev((y + o) % ny, x, zh * 2 + cc))
    greet(sibling)
    greet(partner)
    greet(up)
    greet(down)
    greet(right)
    greet(far)
    greet(left)
    greet((dp, (ctx + 1) % n_ctx, tp))
    greet((dp, (ctx + n_ctx - 1) % n_ctx, tp))

    cut = rows * 3 // 4
    part = rows - cut
    load_k.wait()
    load_v.wait()
    for j in range(half):
        lo = HD * j
        kvs[j, 0:rows] = jnp.concatenate(
            [k_ref[:, lo : lo + HD], v_ref[:, lo : lo + 32]], axis=1
        )
        kvs[j, rows : rows + rows // 2] = jnp.concatenate(
            [v_ref[0 : rows // 2, lo + 32 : lo + HD], v_ref[rows // 2 : rows, lo + 32 : lo + HD]],
            axis=1,
        )

    pl.semaphore_wait(barrier, 2 * (ny - 1) + 9)

    def rank(distance):
        sign = distance // (half + 1)
        fold = distance + sign * (ny - 2 * distance)
        odd = distance % 2
        return odd * (fold // 2 * 2 + sign) + (1 - odd) * (fold // 2 + fold // half + sign)

    near = [0]
    for o in range(1, half):
        near += [o, ny - o]
    near.append(half)

    def to_head(o, src, dst, send_sem, recv_sem):
        head = (y + o) % ny
        j = head % half
        device = dev(head, x, zh * 2 + parity)

        @pl.when(head // half == core)
        def _():
            if o == 0:
                send_or_keep(core == parity, src.at[j], dst, send_sem.at[j], recv_sem, device)
            else:
                send(src.at[j], dst, send_sem.at[j], recv_sem, device)

    def kv_to_head(o):
        place = rank((ny - o) % ny)
        to_head(o, kvs, kvbuf.at[x, place], skv_s, kv_r.at[x, place])

    for o in near[:3]:
        kv_to_head(o)
    pieces = wa_s.shape[0]
    piece_rows = w_ref.shape[0] // pieces

    def piece_of(ref, i):
        return ref.at[i * piece_rows : (i + 1) * piece_rows]

    low, high = dp == 0, dp == n_dp - 1
    edge = jnp.logical_or(low, high)

    def relay(i):
        held = piece_of(wall.at[away], i)

        @pl.when(edge)
        def _():
            wait_for(held, w_r.at[i])

        for on, device in ((low, up), (high, down)):

            @pl.when(on)
            def _():
                send(held, held, wb_s.at[i], w_r.at[i], device)

    def share(i):
        held = piece_of(wall.at[away], i)

        @pl.when(jnp.logical_not(edge))
        def _():
            wait_for(held, w_r.at[i])

        send(held, held, wf_s.at[i], wf_r.at[i], sibling)

    load_q.wait()
    for j in range(half):
        lo = HD * j
        qs[j] = jnp.concatenate(
            [
                q_ref[0:cut, lo : lo + HD],
                jnp.concatenate(
                    [q_ref[cut:rows, lo + 32 * i : lo + 32 * (i + 1)] for i in range(3)], axis=0
                ),
            ],
            axis=1,
        )
    for o in near[::-1]:
        to_head(o, qs, qbuf.at[y], sq_s, q_r.at[y])
    for o in near[3:]:
        kv_to_head(o)

    for on, device in ((low, down), (high, up)):

        @pl.when(on)
        def _():
            for i in range(pieces):
                src, dst = piece_of(w_ref, i), piece_of(wall.at[tp], i)
                send(src, dst, wa_s.at[i], w_r.at[i], device)

    def spread(s):
        wait_for(kvbuf.at[x, s], kv_r.at[x, s])
        send(kvbuf.at[x, s], kvbuf.at[x, s], xr_s.at[s], kv_r.at[x, s], right)
        send(kvbuf.at[x, s], kvbuf.at[x, s], xl_s.at[s], kv_r.at[x, s], left)
        send(kvbuf.at[x, s], kvbuf.at[x, s], xf_s.at[s], kv_r.at[x, s], far)

    def arrive(slot, s):
        wait_for(kvbuf.at[slot, s], kv_r.at[slot, s])

    span = graw.shape[0] // half

    def relayout(i):
        @pl.loop(0, span // 16)
        def _(r):
            at = pl.ds(pl.multiple_of(i * span + r * 16, 16), 16)
            pair = graw[at].astype(F32)
            gw[at] = jnp.concatenate([pair[:, 0, :], pair[:, 1, :]], axis=1).astype(BF16)

    spread(0)
    for i in range(half):
        ys = 2 * ((y // 2 + i + 1) % half) + core
        wait_for(qbuf.at[ys], q_r.at[ys])
        send(qbuf.at[ys], qbuf.at[ys], qf_s.at[i], q_r.at[ys], sibling)
    own_g.wait()
    relayout(0)
    relay(0)
    spread(1)
    send(w_ref, wall.at[tp], w_s, ww_r, sibling)
    relayout(1)
    for i in range(half):
        ys = 2 * ((y // 2 + i) % half) + 1 - core
        wait_for(qbuf.at[ys], q_r.at[ys])

    @pl.loop(0, ny)
    def _(t):
        base = pl.multiple_of(t * rows, rows)
        qfull[pl.ds(base, cut)] = jnp.concatenate(
            [qbuf[t, :, 0:HD], jnp.zeros((cut, LANES - HD), BF16)], axis=1
        )
        qfull[pl.ds(base + cut, part)] = jnp.concatenate(
            [qbuf[t, part * i : part * (i + 1), HD:LANES] for i in range(3)]
            + [jnp.zeros((part, LANES - HD), BF16)],
            axis=1,
        )

    relayout(2)
    factor = math.log2(math.e) / math.sqrt(HD)
    hr_rows = rows // 2
    tall = rows + hr_rows

    quarter = half // 2

    def unpack(slots, first_place):
        ones = jnp.ones((hr_rows, LANES - HD), BF16)
        for n, slot in enumerate(slots):
            for m in range(quarter):
                for b in range(2):
                    base = (n * quarter + m) * rows + b * hr_rows
                    vfull[base : base + hr_rows] = jnp.concatenate(
                        [
                            kvbuf[slot, first_place + m, b * hr_rows : (b + 1) * hr_rows, HD:LANES],
                            kvbuf[slot, first_place + m, rows:tall, 64 * b : 64 * (b + 1)],
                            ones,
                        ],
                        axis=1,
                    )

    wide = 2 * rows

    def tile(slots, place, base, first):
        at = pl.ds(pl.multiple_of(base, wide), wide)
        kk = jnp.concatenate(
            [
                kvbuf[slot, place : place + quarter, 0:rows, :].reshape(quarter * rows, LANES)
                for slot in slots
            ],
            axis=0,
        )
        s = lax.dot_general(
            qfull[at], kk, (((1,), (1,)), ((), ())), preferred_element_type=F32
        )
        peak = jnp.max(s, axis=1, keepdims=True) * factor
        if first:
            new = peak
        else:
            old = top[at][:, 0:1]
            new = jnp.maximum(old, peak)
        p = jnp.exp2(s * factor - new)
        mix = jnp.dot(p.astype(BF16), vfull[...], preferred_element_type=F32)
        if not first:
            mix = mix + acc[at] * jnp.exp2(old - new)
        return at, mix, new

    def attend(slots, place, first):
        unpack(slots, place)
        for t in range(half):
            at, mix, new = tile(slots, place, t * wide, first)
            acc[at] = mix
            top[at] = jnp.broadcast_to(new, (wide, LANES))

    relay(1)
    arrive(x_left, 0)
    arrive(x_left, 1)
    attend((x, x_left), 0, True)
    relay(2)
    spread(2)
    relayout(3)
    spread(3)
    arrive(x_right, 0)
    arrive(x_right, 1)
    arrive(x_far, 0)
    arrive(x_far, 1)
    attend((x_right, x_far), 0, False)
    relay(3)
    arrive(x_left, 2)
    arrive(x_left, 3)
    attend((x, x_left), 2, False)
    relay(4)
    arrive(x_right, 2)
    arrive(x_right, 3)
    arrive(x_far, 2)
    arrive(x_far, 3)
    last = (x_right, x_far)
    unpack(last, 2)
    lane = lax.broadcasted_iota(jnp.int32, (wide, LANES), 1)
    for t in range(half // 2):
        at, mix, new = tile(last, 2, (1 - core) * half * rows + t * wide, False)
        acc[at] = jnp.where(lane >= LANES - 16, jnp.broadcast_to(new, (wide, LANES)), mix)
        send(acc.at[at], accr.at[pl.ds(t * wide, wide)], a_s.at[t], a_r.at[t], sibling)
    for t in range(half // 2):
        at, mix, new = tile(last, 2, core * half * rows + t * wide, False)
        acc[at] = mix
        top[at] = jnp.broadcast_to(new, (wide, LANES))
    relay(5)
    for i in range(2):
        share(i)
    for t in range(half // 2):
        wait_for(accr.at[pl.ds(t * wide, wide)], a_r.at[t])
        for k in range(2 * t, 2 * t + 2):
            yd = core * half + k
            at = pl.ds(pl.multiple_of(yd * rows, rows), rows)
            other = accr[k * rows : (k + 1) * rows]
            other_top = other[:, LANES - 1 : LANES]
            new = top[at][:, 0:1]
            both = jnp.maximum(new, other_top)
            total = acc[at] * jnp.exp2(new - both) + other * jnp.exp2(other_top - both)
            out = (total / total[:, HD : HD + 1]).astype(BF16)
            for cc in range(2):
                for zz in range(2):
                    src = (zz * 2 + cc) * block
                    ctxs[k, cc, zz * block : (zz + 1) * block] = out[src : src + block]
            for cc in range(2):
                send_or_keep(
                    jnp.logical_and(yd == y, core == cc),
                    ctxs.at[k, cc],
                    cbuf.at[y],
                    c_s.at[k, cc],
                    c_r.at[y],
                    dev(yd, x, zh * 2 + cc),
                )

    share(2)
    share(3)
    for load in (own_w, own_x, own_x2, load_gain, load_bias):
        load.wait()
    wait_for(wall.at[zh * 2 + 1 - core], ww_r)
    total = resid[...].astype(F32)
    for g in range(2):
        for j in range(half):
            wait_for(cbuf.at[g * half + j], c_r.at[g * half + j])
            cat[zh, g, :, HD * j : HD * (j + 1)] = cbuf[g * half + j, :, 0:HD]
        send(cat.at[zh, g], cat.at[zh, g], z_s.at[g], z_r.at[g], partner)
    for g in range(2):
        total += jnp.dot(cat[zh, g], wall[zh * 2 + g], preferred_element_type=F32)
    for i in range(4, pieces):
        share(i)
    for i in range(pieces):
        wait_for(piece_of(wall.at[away_sibling], i), wf_r.at[i])
    for g in range(2):
        wait_for(cat.at[1 - zh, g], z_r.at[g])
        total += jnp.dot(cat[1 - zh, g], wall[(1 - zh) * 2 + g], preferred_element_type=F32)
    attended = total.astype(BF16)
    resid[...] = attended
    att_ref[...] = resid[pl.ds(pl.multiple_of(zh * block, block), block)]
    full = attended.astype(F32)
    centred = full - jnp.mean(full, axis=1, keepdims=True)
    var = jnp.mean(centred * centred, axis=1, keepdims=True)
    normed = centred * lax.rsqrt(var + 1e-05) * gain_ref[...].reshape(1, -1)
    nbuf[core] = (normed + bias_ref[...].reshape(1, -1)).astype(BF16)
    send(nbuf.at[core], nbuf.at[core], n_s, n_r, sibling)

    def gate(cc):
        projected = jnp.dot(nbuf[cc], gw[...], preferred_element_type=F32)
        gated = projected[:, 0:width] * jax.nn.sigmoid(projected[:, width:])
        gated = gated.astype(BF16).astype(F32)
        for zz in range(2):
            base = pl.multiple_of(rim + (zz * 2 + cc) * block, 16)
            gpad[pl.ds(base, block)] = gated[zz * block : (zz + 1) * block]
        edge = pl.multiple_of(rim + cc * (rows - rim), 16)
        hs[cc] = gpad[pl.ds(edge, rim)].astype(BF16)
        target = ctx + 2 * cc - 1

        @pl.when(jnp.logical_and(target >= 0, target < n_ctx))
        def _():
            send(hs.at[cc], hr.at[1 - cc], h_s.at[cc], h_r.at[1 - cc], (dp, target, tp))

    gate(core)
    wait_for(nbuf.at[1 - core], n_r)
    gate(1 - core)

    for side in range(2):
        source = ctx + 2 * side - 1
        exists = jnp.logical_and(source >= 0, source < n_ctx)
        place = pl.ds(side * (rim + rows), rim)

        @pl.when(exists)
        def _():
            wait_for(hr.at[side], h_r.at[side])
            gpad[place] = hr[side].astype(F32)

        @pl.when(jnp.logical_not(exists))
        def _():
            gpad[place] = jnp.zeros((rim, width), F32)

    for j in range(half):
        here = jnp.logical_and(core * half + j == y, core == parity)

        @pl.when(jnp.logical_not(here))
        def _():
            wait_for(qs.at[j], sq_s.at[j])
            wait_for(kvs.at[j], skv_s.at[j])

        wait_for(qbuf.at[j], qf_s.at[j])
        wait_for(kvbuf.at[x, j], xr_s.at[j])
        wait_for(kvbuf.at[x, j], xl_s.at[j])
        wait_for(kvbuf.at[x, j], xf_s.at[j])
        for cc in range(2):

            @pl.when(jnp.logical_not(jnp.logical_and(core * half + j == y, core == cc)))
            def _():
                wait_for(ctxs.at[j, cc], c_s.at[j, cc])

    wait_for(wall.at[tp], w_s)
    for t in range(half // 2):
        wait_for(accr.at[pl.ds(t * wide, wide)], a_s.at[t])
    for i in range(pieces):
        wait_for(piece_of(w_ref, i), wf_s.at[i])

        @pl.when(edge)
        def _():
            wait_for(piece_of(w_ref, i), wa_s.at[i])
            wait_for(piece_of(w_ref, i), wb_s.at[i])

    for g in range(2):
        wait_for(cat.at[zh, g], z_s.at[g])
    wait_for(nbuf.at[core], n_s)
    for side in range(2):
        target = ctx + 2 * side - 1

        @pl.when(jnp.logical_and(target >= 0, target < n_ctx))
        def _():
            wait_for(hs.at[side], h_s.at[side])


def convolve(att_in, gpad, taps_ref, scale_ref, shift_ref, att_ref, conv_ref):
    rows = conv_ref.shape[0]
    rim = (gpad.shape[0] - rows) // 2
    att_ref[...] = att_in[...]
    offset = rim - (KERNEL - 1) // 2
    taps = taps_ref[...]
    scale = scale_ref[...].reshape(1, -1)
    shift = shift_ref[...].reshape(1, -1)

    for r in range(0, rows, 4 * rim):
        for lane in range(0, conv_ref.shape[1], LANES):
            at = slice(lane, lane + LANES)
            window = gpad[r : r + 6 * rim, at]
            total = None
            for turn in range(8):
                places = [p for p in range(offset, offset + KERNEL) if p % 8 == turn]
                top = places[-1] + 4 * rim
                turned = window[turn : turn + (top - turn) // 8 * 8]
                for p in places:
                    term = turned[p - turn : p - turn + 4 * rim] * taps[p - offset : p - offset + 1, at]
                    total = term if total is None else total + term
            u = total * scale[:, at] + shift[:, at]
            conv_ref[r : r + 4 * rim, at] = (u * jax.nn.sigmoid(u)).astype(BF16)


def shards(
    n_ctx,
    residual_in,
    queries,
    keys,
    values,
    out_weight,
    norm_gain,
    norm_bias,
    glu_weight,
    conv_weight,
    conv_scale,
    conv_shift,
):
    rows, columns = queries.shape
    half = columns // HD
    ny = 2 * half
    nx = n_ctx // ny
    model = residual_in.shape[1]
    block = rows // 4
    pieces = columns // 64
    rim = 16
    vmem = pl.BlockSpec(memory_space=pltpu.VMEM)
    anywhere = pl.BlockSpec(memory_space=pl.ANY)
    dma = pltpu.SemaphoreType.DMA
    tall = rows + rows // 2
    scratch = [
        pltpu.VMEM((rows, columns), BF16),
        pltpu.VMEM((rows, columns), BF16),
        pltpu.VMEM((rows, columns), BF16),
        pltpu.VMEM((model,), F32),
        pltpu.VMEM((model,), F32),
        pltpu.VMEM((half, rows * 3 // 4, LANES), BF16),
        pltpu.VMEM((half, tall, LANES), BF16),
        pltpu.VMEM((ny, rows * 3 // 4, LANES), BF16),
        pltpu.VMEM((nx, half, tall, LANES), BF16),
        pltpu.VMEM((ny * rows, LANES), BF16),
        pltpu.VMEM((half * rows, LANES), BF16),
        pltpu.VMEM((ny * rows, LANES), F32),
        pltpu.VMEM((ny * rows, LANES), F32),
        pltpu.VMEM((half * rows, LANES), F32),
        pltpu.VMEM((half, 2, 2 * block, LANES), BF16),
        pltpu.VMEM((ny, 2 * block, LANES), BF16),
        pltpu.VMEM((2, 2, 2 * block, columns), BF16),
        pltpu.VMEM((4, columns, model), BF16),
        pltpu.VMEM((model, 2, columns), BF16),
        pltpu.VMEM((model, 2 * columns), BF16),
        pltpu.VMEM((2 * block, model), BF16),
        pltpu.VMEM((2, 2 * block, model), BF16),
        pltpu.VMEM((2, rim, columns), BF16),
        pltpu.VMEM((2, rim, columns), BF16),
        dma((half,)),
        dma((half,)),
        dma((ny,)),
        dma((half,)),
        dma((nx, half)),
        dma((half,)),
        dma((half,)),
        dma((half,)),
        dma((half,)),
        dma((half,)),
        dma((half, 2)),
        dma((ny,)),
        dma,
        dma,
        dma((9,)),
        dma((2,)),
        dma((2,)),
        dma,
        dma,
        dma((pieces,)),
        dma((pieces,)),
        dma((pieces,)),
        dma((pieces,)),
        dma((pieces,)),
        dma((2,)),
        dma((2,)),
    ]
    attended, padded = pl.pallas_call(
        functools.partial(kernel, ny, nx),
        out_shape=(
            jax.ShapeDtypeStruct((block, model), BF16),
            jax.ShapeDtypeStruct((rows + 2 * rim, columns), F32),
        ),
        in_specs=[anywhere] * 8,
        out_specs=(vmem, vmem),
        scratch_shapes=scratch,
        compiler_params=pltpu.CompilerParams(
            collective_id=0, has_side_effects=True, vmem_limit_bytes=56 * 1024 * 1024
        ),
        cost_estimate=pl.CostEstimate(
            flops=3 * 10**9, bytes_accessed=10**7, transcendentals=5 * 10**6
        ),
    )(
        residual_in,
        queries,
        keys,
        values,
        out_weight,
        norm_gain,
        norm_bias,
        glu_weight,
    )
    return pl.pallas_call(
        convolve,
        out_shape=(
            jax.ShapeDtypeStruct((block, model), BF16),
            jax.ShapeDtypeStruct((rows, columns), BF16),
        ),
        in_specs=[vmem] * 5,
        out_specs=(vmem, vmem),
    )(attended, padded, conv_weight, conv_scale, conv_shift)


def solution(mesh):
    return jax.shard_map(
        functools.partial(shards, mesh.shape["ctx"]),
        mesh=mesh,
        in_specs=(
            P(("dp", "ctx"), None),
            P(("dp", "ctx"), "tp"),
            P(("dp", "ctx"), "tp"),
            P(("dp", "ctx"), "tp"),
            P("tp", None),
            P(),
            P(),
            P(None, None, "tp"),
            P(None, "tp"),
            P("tp"),
            P("tp"),
        ),
        out_specs=(P(("dp", "ctx", "tp"), None), P(("dp", "ctx"), "tp")),
        check_vma=False,
    )
```
